1024 devices in a mesh: group: 64 (over x, z), tensor: 16 (over y, core).
Axes of the slice: x: 4, y: 8, z: 16, core: 2. Of those that a mesh axis runs over, the one named last changes fastest.
Arguments:
- pre_hidden: bfloat16 [9216, 8192], P('group', 'tensor'), may hold values from -6 to 6
- proj_weight: bfloat16 [8192, 8192], P('tensor'), may hold values from -0.09375 to 0.09375
- text_embed: bfloat16 [24576, 8192], P('group', 'tensor'), may hold values from -6 to 6
- routes_dest: int32 [9216, 1], P('group'), may hold values from 0 to 63; in each aligned block of 144 rows (0 to 143, 144 to 287, ...) at most 3 rows name the same one
- place: int32 [64, 192], P('group'), may hold values from 0 to 383, as said below
- grad_packed: bfloat16 [24576, 8192], P('group', 'tensor'), may hold values from -6 to 6
Outputs:
- packed: bfloat16 [24576, 8192], P('group', 'tensor')
- grad_hidden: bfloat16 [9216, 8192], P('group', 'tensor')
The draws below stay inside these ranges and needn't reach their ends.
Inputs may be any that keep to these rules, and one draw needn't show every extreme that they name: `routes_dest`: no destination is named by more than 3 image tokens of one owner, a bound that some block reaches. `place`: the offsets of one row are all different.
All inputs are finite; a program needn't handle non-finite values.
Results may differ from the reference program's by a relative error of at most 0.012.
Values may be sent and summed in bfloat16 or wider, within the bound.
No kernel may reach another device: no remote copies, remote signals or barrier semaphores. Data moves between devices by JAX's collectives and lax.ppermute only.
A program may use at most 64 MiB of HBM per device.

```python
import math
import jax
import jax.numpy as jnp
import numpy as np
from jax import lax

D = 8192
HID = 8192
ROWS_DEV = 144
CAP = 3
SLOTS = 192
SEQ_DEV = 384
ROWS = 9216
SEQ = 24576
N_GROUP = 64
N_TENSOR = 16


def draw_place(key, part):
    key = jax.random.fold_in(key, 7)
    keys = jax.random.split(key, N_GROUP)

    def one_row(row_key):
        perm_key, bit_key = jax.random.split(row_key)
        order = jax.random.permutation(perm_key, SLOTS).astype(jnp.int32)
        bits = jax.random.randint(bit_key, (SLOTS,), 0, 2).astype(jnp.int32)
        bits = jnp.where(order == SLOTS - 1, 1, bits)
        bits = jnp.where(order == 0, 0, bits)
        return (2 * order + bits).astype(jnp.int32)
    return jax.vmap(one_row)(keys)


def spiked(entries, key, source, target, shards_of, factor):
    def block_of(axis_at):
        return (jnp.arange(entries.shape[axis_at]) // (entries.shape[axis_at] // shards_of)).reshape((-1,) + (1,) * (entries.ndim - 1 - axis_at))

    first = jax.random.permutation(key, shards_of)[block_of(target)]
    second = (block_of(target) + shards_of // 2) % shards_of
    return jnp.where((block_of(source) == first) | (block_of(source) == second), factor * entries, entries)


def block_levels(key, dims, shards, low, top_value):
    def one(position, parts):
        heights = jax.random.uniform(jax.random.fold_in(jax.random.fold_in(key, 6), position), (parts,), jnp.float32, low / len(shards), top_value / len(shards))
        return jnp.repeat(jnp.exp(heights), dims[position] // parts).reshape((-1,) + (1,) * (len(dims) - position - 1))

    level = one(*shards[0])
    for cut in shards[1:]:
        level = level * one(*cut)
    return level


def shared_out(rng, own, number, rows, count, top, bound, lean):
    sequence = jax.random.permutation(rng, count)
    crowded, common = shares(count, rows * top, bound, lean, True), shares(count, rows * top, bound, lean, False)
    places = jnp.arange(count)

    def named(tallies, turn):
        used = int((tallies > 0).sum())
        fixed = max(1, used // 4)
        shifted = fixed + (places - fixed + turn * (used - fixed)) % max(1, count - fixed)
        return jnp.zeros((count,), jnp.int32).at[sequence[jnp.where(places < fixed, places, shifted)]].set(jnp.asarray(tallies, jnp.int32))

    tallies = jnp.where(number % 4 == 0, named(crowded, number // 4), named(common, number - number // 4 - 1))
    mixed = jax.random.permutation(jax.random.fold_in(own, 3), count)
    source_of, sink = mixed[0:count // 2 * 2:2], mixed[1:count // 2 * 2:2]
    margin = jnp.minimum(tallies[source_of] - 1, bound - tallies[sink]) // 2
    margin = jnp.where((source_of == sequence[0]) | (sink == sequence[0]) | (tallies[sink] == 0), 0, jnp.maximum(margin, 0))
    shifted = jax.random.randint(jax.random.fold_in(own, 4), (count // 2,), 0, 1 << 20) % (margin + 1)
    tallies = tallies.at[source_of].add(-shifted).at[sink].add(shifted)
    labels = jnp.searchsorted(jnp.cumsum(tallies), jnp.arange(rows * top), side="right").astype(jnp.int32)
    grid = labels.reshape(top, rows).T
    grid = grid[jax.random.permutation(jax.random.fold_in(own, 1), rows)]
    turn = jax.random.randint(jax.random.fold_in(own, 2), (rows, 1), 0, top)
    return jnp.take_along_axis(grid, (jnp.arange(top)[None, :] + turn) % top, axis=1)


def shares(count, total, most, slope, full):
    portions = [(1 << 20) // math.isqrt(rank ** slope) + 1 for rank in range(1, count + 1)]
    largest = most if full else min(most, max(-(-total // count), total * portions[0] // sum(portions)))
    least = 1 if total - largest >= count - 1 else 0
    holding, surplus = [largest] + [least] * (count - 1), total - largest - least * (count - 1)
    while surplus > 0:
        free = [i for i in range(1, count) if holding[i] < largest] or [i for i in range(1, count) if holding[i] < most]
        mass, budget = sum([portions[i] for i in free]), surplus
        for i in free:
            extra = min(most - holding[i], max(1, budget * portions[i] // mass), surplus)
            holding[i] = holding[i] + extra
            surplus = surplus - extra
    return np.array(holding)


def gaussian(own_key, shape, spread, bound, cuts=(), kind=jnp.bfloat16):
    drawn = jax.random.normal(own_key, shape, jnp.float32) * spread
    if len(cuts) > 0:
        drawn = block_levels(own_key, shape, cuts, -0.22, 0.18) * drawn
    return jnp.clip(drawn, min=-bound, max=bound).astype(kind)


def gaussian_with(own_key, shape, scale, reach, cuts, heavy, kind=jnp.bfloat16):
    drawn = scale * jax.random.normal(own_key, shape, jnp.float32)
    if cuts:
        drawn = drawn * block_levels(own_key, shape, cuts, -0.22, 0.18)
    return jnp.clip(spiked(drawn, jax.random.fold_in(own_key, 3), *heavy), -reach, reach).astype(kind)


def setup_inputs(seed: int = 0) -> dict:
    splits = jax.random.split(jax.random.key(seed), 7)
    pre_hidden = gaussian(splits[0], (ROWS, HID), 1.0, 6.0, ((0, 64), (1, 16)))
    proj_weight = gaussian_with(splits[1], (HID, D), HID ** -0.5, 0.09375, ((0, 16),), (0, 1, 16, 2.0))
    text_embed = gaussian(splits[2], (SEQ, D), 1.0, 6.0, ((0, 64), (1, 16)))
    routes_dest_keys = jax.random.split(jax.random.fold_in(splits[3], 1), ROWS // ROWS_DEV)
    routes_dest_turns = jax.random.permutation(jax.random.fold_in(splits[3], 3), ROWS // ROWS_DEV)
    routes_dest = jax.vmap(lambda own, number: shared_out(jax.random.fold_in(splits[3], 2), own, number, ROWS_DEV, N_GROUP, 1, CAP, 2))(routes_dest_keys, routes_dest_turns).reshape((ROWS, 1))
    place = draw_place(jax.random.fold_in(splits[6], 71), 0)
    grad_packed = gaussian(splits[5], (SEQ, D), 1.0, 6.0, ((0, 64), (1, 16)))
    return dict(pre_hidden=pre_hidden, proj_weight=proj_weight, text_embed=text_embed, routes_dest=routes_dest, place=place, grad_packed=grad_packed)


def gelu_slope(values):
    cdf = 0.5 * (1.0 + jax.scipy.special.erf(values * 0.7071067811865476))
    dens = jnp.exp(-0.5 * values * values) * 0.3989422804014327
    return cdf + values * dens


def reference(pre_hidden, proj_weight, text_embed, routes_dest, place, grad_packed):
    pre_float = pre_hidden.astype(jnp.float32)
    act = jax.nn.gelu(pre_float, approximate=False).astype(jnp.bfloat16)
    width = HID // N_TENSOR

    def add_block(index, total):
        start = (index * width).astype(jnp.int32)
        act_block = lax.dynamic_slice_in_dim(act, start, width, 1)
        weight_block = lax.dynamic_slice_in_dim(proj_weight, start, width, 0)
        term = jnp.dot(act_block, weight_block, preferred_element_type=jnp.float32).astype(jnp.bfloat16)
        term = lax.optimization_barrier(term)
        return total + term.astype(jnp.float32)

    embed = lax.fori_loop(0, N_TENSOR, add_block, jnp.zeros((ROWS, D), jnp.float32)).astype(jnp.bfloat16)
    dest = routes_dest[:, 0].reshape(N_GROUP, ROWS_DEV).astype(jnp.int32)
    onehot = (dest[:, :, None] == jnp.arange(N_GROUP, dtype=jnp.int32)[None, None, :]).astype(jnp.int32)
    ranks = jnp.sum(jnp.where(onehot == 1, jnp.cumsum(onehot, axis=1) - 1, 0), axis=2).astype(jnp.int32)
    owners = jnp.arange(N_GROUP, dtype=jnp.int32)[:, None]
    spots = place[dest, owners * CAP + ranks].astype(jnp.int32)
    positions = (dest * SEQ_DEV + spots).reshape(-1).astype(jnp.int32)
    packed = text_embed.at[positions].set(embed)
    grad_rows = grad_packed[positions]
    grad_act = lax.dot_general(grad_rows, proj_weight, (((1,), (1,)), ((), ())), preferred_element_type=jnp.float32)
    grad_hidden = (grad_act * gelu_slope(pre_float)).astype(jnp.bfloat16)
    return packed, grad_hidden
```

```python
import functools

import jax
import jax.numpy as jnp
from jax import lax
from jax.experimental import pallas as pl
from jax.experimental.pallas import tpu as pltpu
from jax.sharding import Mesh
from jax.sharding import PartitionSpec as P

BF16 = jnp.bfloat16
F32 = jnp.float32
EMPTY = 1.7e38
LIMIT = 1.0e38


def gelu(values):
    return values * 0.5 * (1.0 + lax.erf(values * 0.7071067811865476))


def gelu_slope(values):
    cdf = 0.5 * (1.0 + lax.erf(values * 0.7071067811865476))
    dens = jnp.exp(-0.5 * values * values) * 0.3989422804014327
    return cdf + values * dens


def rows_by_target(dest_row, groups, capacity, slots):
    rows = dest_row.shape[1]
    hit = lax.broadcasted_iota(jnp.int32, (groups, rows), 0) == dest_row
    before = lax.broadcasted_iota(jnp.int32, (rows, rows), 0) < lax.broadcasted_iota(
        jnp.int32, (rows, rows), 1
    )
    onehot = jnp.where(hit, 1.0, 0.0)
    counts = jnp.dot(
        onehot.astype(BF16), jnp.where(before, 1.0, 0.0).astype(BF16), preferred_element_type=F32
    )
    rank = jnp.sum(onehot * counts, axis=0, keepdims=True).astype(jnp.int32)
    target = dest_row * capacity + rank
    return lax.broadcasted_iota(jnp.int32, (slots, rows), 0) == target


def gather_kernel(offsets_ref, grad_ref, out_ref):
    length, slots = grad_ref.shape[0], offsets_ref.shape[1]
    pick = lax.broadcasted_iota(jnp.int32, (length, slots), 0) == offsets_ref[...]
    pick = jnp.where(pick, 1.0, 0.0).astype(BF16)
    out_ref[...] = lax.dot_general(
        pick, grad_ref[...], (((0,), (0,)), ((), ())), preferred_element_type=F32
    ).astype(BF16)


def owner_rows_kernel(groups, capacity, dest_ref, arrived_ref, out_ref):
    slots = arrived_ref.shape[0]
    pick = rows_by_target(dest_ref[...], groups, capacity, slots)
    pick = jnp.where(pick, 1.0, 0.0).astype(BF16)
    rows = lax.dot_general(
        pick, arrived_ref[...], (((0,), (0,)), ((), ())), preferred_element_type=F32
    ).astype(BF16)
    for j in range(out_ref.shape[0]):
        out_ref[j] = rows


def route_kernel(groups, capacity, dest_ref, terms_ref, out_ref):
    slots = out_ref.shape[0]
    total = terms_ref[0].astype(F32)
    for j in range(1, terms_ref.shape[0]):
        total += terms_ref[j].astype(F32)
    hit = rows_by_target(dest_ref[...], groups, capacity, slots)
    pick = jnp.where(hit, 1.0, 0.0)
    sent = jnp.dot(pick.astype(BF16), total.astype(BF16), preferred_element_type=F32)
    used = jnp.sum(pick, axis=1, keepdims=True)
    out_ref[...] = jnp.where(used > 0.5, sent, EMPTY).astype(BF16)


def place_kernel(offsets_ref, arrived_ref, text_ref, out_ref):
    length, slots = text_ref.shape[0], offsets_ref.shape[1]
    arrived = arrived_ref[...].astype(F32)
    used = arrived[:, 0:1] < LIMIT
    rows = jnp.where(used, arrived, 0.0).astype(BF16)
    marks = jnp.where(jnp.broadcast_to(used, (slots, 128)), 1.0, 0.0).astype(BF16)
    pick = lax.broadcasted_iota(jnp.int32, (length, slots), 0) == offsets_ref[...]
    pick = jnp.where(pick, 1.0, 0.0).astype(BF16)
    placed = jnp.dot(pick, rows, preferred_element_type=F32)
    filled = jnp.dot(pick, marks, preferred_element_type=F32)[:, 0:1] > 0.5
    out_ref[...] = jnp.where(filled, placed, text_ref[...].astype(F32)).astype(BF16)


def forward_first_kernel(at_ref, own_ref, other_ref, w_own_ref, w_other_ref, out_ref, act_ref):
    half = own_ref.shape[1]

    @pl.when(pl.program_id(0) == 0)
    def _():
        act_ref[:, :half] = gelu(own_ref[...].astype(F32)).astype(BF16)
        act_ref[:, half:] = gelu(other_ref[...].astype(F32)).astype(BF16)

    total = jnp.dot(act_ref[:, :half], w_own_ref[...], preferred_element_type=F32)
    total += jnp.dot(act_ref[:, half:], w_other_ref[...], preferred_element_type=F32)
    out_ref[0] = total.astype(BF16)


def forward_second_kernel(at_ref, act_ref, w_own_ref, w_other_ref, out_ref):
    half = w_own_ref.shape[0]
    total = jnp.dot(act_ref[:, :half], w_own_ref[...], preferred_element_type=F32)
    total += jnp.dot(act_ref[:, half:], w_other_ref[...], preferred_element_type=F32)
    out_ref[0] = total.astype(BF16)


TRANS = (((1,), (1,)), ((), ()))


def backward_first_kernel(at_ref, grad_ref, w_own_ref, w_other_ref, own_ref, other_ref):
    own = lax.dot_general(grad_ref[0], w_own_ref[...], TRANS, preferred_element_type=F32)
    other = lax.dot_general(grad_ref[0], w_other_ref[...], TRANS, preferred_element_type=F32)

    @pl.when(pl.program_id(0) == 0)
    def _():
        own_ref[...] = own
        other_ref[...] = other

    @pl.when(pl.program_id(0) > 0)
    def _():
        own_ref[...] += own
        other_ref[...] += other


def backward_second_kernel(
    at_ref, grad_ref, w_own_ref, w_other_ref, own_in, other_in, own_ref, other_ref, total_ref
):
    own = lax.dot_general(grad_ref[0], w_own_ref[...], TRANS, preferred_element_type=F32)
    other = lax.dot_general(grad_ref[0], w_other_ref[...], TRANS, preferred_element_type=F32)

    @pl.when(pl.program_id(0) == 0)
    def _():
        own_ref[...] = own_in[...] + own
        total_ref[...] = other_in[...] + other

    @pl.when(pl.program_id(0) > 0)
    def _():
        own_ref[...] += own
        total_ref[...] += other

    @pl.when(pl.program_id(0) == pl.num_programs(0) - 1)
    def _():
        other_ref[...] = total_ref[...].astype(BF16)


def slope_kernel(own_ref, other_ref, pre_ref, out_ref):
    total = own_ref[...] + other_ref[...].astype(F32)
    out_ref[...] = (total * gelu_slope(pre_ref[...].astype(F32))).astype(BF16)


def call(kernel, out, *args, **kw):
    return pl.pallas_call(kernel, out_shape=jax.ShapeDtypeStruct(*out), **kw)(*args)


def on_device(lines, pre_hidden, proj_weight, text_embed, routes_dest, place, grad_packed):
    groups = lax.axis_size("group")
    slots = place.shape[1]
    capacity = slots // groups
    rows, hid = pre_hidden.shape
    width = text_embed.shape[1]
    half = lines // 2
    line, core = lax.axis_index("line"), lax.axis_index("core")
    parity = lax.rem(line, 2)
    same = (2 * parity + core).astype(jnp.int32).reshape(1)
    opposite = (2 * (1 - parity) + core).astype(jnp.int32).reshape(1)
    dest_row = routes_dest.reshape(1, rows)

    cores = [(0, 1), (1, 0)]
    beside = []
    for i in range(lines):
        for c in range(2):
            odd = (i + c) % 2
            beside.append((2 * i + c, 2 * ((i + (-1 if odd else 1)) % lines) + c))
    alike = [list(range(0, lines, 2)), list(range(1, lines, 2))]

    def exchange(x):
        return lax.all_to_all(
            x.reshape(groups, capacity, width), "group", split_axis=0, concat_axis=0, tiled=True
        ).reshape(slots, width)

    slot_grad = call(gather_kernel, ((slots, width), BF16), place, grad_packed)
    returned = exchange(slot_grad)

    pre_other = lax.ppermute(pre_hidden, "core", cores)
    w_other = lax.ppermute(proj_weight, "core", cores)

    w_spec = pl.BlockSpec((hid, width), lambda j, at: (0, 4 * j + at[0]))
    whole = lambda shape: pl.BlockSpec(shape, lambda j, at: (0,) * len(shape))
    term = pl.BlockSpec((1, rows, width), lambda j, at: (j, 0, 0))
    flops = 2 * half * rows * width * 2 * hid
    cost = pl.CostEstimate(flops=flops, bytes_accessed=2 * half * hid * width * 2, transcendentals=0)
    sent, act = pl.pallas_call(
        forward_first_kernel,
        grid_spec=pltpu.PrefetchScalarGridSpec(
            num_scalar_prefetch=1,
            grid=(half,),
            in_specs=[whole((rows, hid)), whole((rows, hid)), w_spec, w_spec],
            out_specs=[term, whole((rows, 2 * hid))],
        ),
        out_shape=[
            jax.ShapeDtypeStruct((half, rows, width), BF16),
            jax.ShapeDtypeStruct((rows, 2 * hid), BF16),
        ],
        cost_estimate=cost,
    )(opposite, pre_hidden, pre_other, proj_weight, w_other)
    beside_terms = lax.ppermute(sent, ("line", "core"), beside)
    kept = pl.pallas_call(
        forward_second_kernel,
        grid_spec=pltpu.PrefetchScalarGridSpec(
            num_scalar_prefetch=1,
            grid=(half,),
            in_specs=[whole((rows, 2 * hid)), w_spec, w_spec],
            out_specs=term,
        ),
        out_shape=jax.ShapeDtypeStruct((half, rows, width), BF16),
        cost_estimate=cost,
    )(same, act, proj_weight, w_other)
    terms = (kept.astype(F32) + beside_terms.astype(F32)).astype(BF16)
    terms = lax.all_to_all(
        terms, "line", split_axis=0, concat_axis=0, tiled=True, axis_index_groups=alike
    )
    outgoing = call(
        functools.partial(route_kernel, groups, capacity), ((slots, width), BF16), dest_row, terms
    )
    arrived = exchange(outgoing)

    mine = call(
        functools.partial(owner_rows_kernel, groups, capacity),
        ((half, rows, width), BF16),
        dest_row,
        returned,
    )
    near = lax.all_to_all(
        mine, "line", split_axis=0, concat_axis=0, tiled=True, axis_index_groups=alike
    )
    far = lax.ppermute(near, ("line", "core"), beside)
    total = whole((rows, hid))
    own, other = pl.pallas_call(
        backward_first_kernel,
        grid_spec=pltpu.PrefetchScalarGridSpec(
            num_scalar_prefetch=1,
            grid=(half,),
            in_specs=[term, w_spec, w_spec],
            out_specs=[total, total],
        ),
        out_shape=[jax.ShapeDtypeStruct((rows, hid), F32)] * 2,
        cost_estimate=cost,
    )(same, near, proj_weight, w_other)
    own, other = pl.pallas_call(
        backward_second_kernel,
        grid_spec=pltpu.PrefetchScalarGridSpec(
            num_scalar_prefetch=1,
            grid=(half,),
            in_specs=[term, w_spec, w_spec, total, total],
            out_specs=[total, total],
            scratch_shapes=[pltpu.VMEM((rows, hid), F32)],
        ),
        out_shape=[
            jax.ShapeDtypeStruct((rows, hid), F32),
            jax.ShapeDtypeStruct((rows, hid), BF16),
        ],
        cost_estimate=cost,
    )(opposite, far, proj_weight, w_other, own, other)
    other = lax.ppermute(other, "core", cores)
    grad_hidden = call(slope_kernel, ((rows, hid), BF16), own, other, pre_hidden)

    packed = call(place_kernel, (text_embed.shape, BF16), place, arrived, text_embed)
    return (packed, grad_hidden)


def solution(mesh):
    groups, lines = mesh.shape["group"], mesh.shape["tensor"] // 2
    chips = Mesh(mesh.devices.reshape(groups, lines, 2), ("group", "line", "core"))
    tensor = ("line", "core")
    return jax.shard_map(
        functools.partial(on_device, lines),
        mesh=chips,
        in_specs=(
            P("group", tensor),
            P(tensor, None),
            P("group", tensor),
            P("group", None),
            P("group", None),
            P("group", tensor),
        ),
        out_specs=(P("group", tensor), P("group", tensor)),
        check_vma=False,
    )
```

```python
import functools

import jax
import jax.numpy as jnp
from jax import lax
from jax.experimental import pallas as pl
from jax.experimental.pallas import tpu as pltpu
from jax.sharding import Mesh
from jax.sharding import PartitionSpec as P

BF16 = jnp.bfloat16
F32 = jnp.float32
EMPTY = 1.7e38
LIMIT = 1.0e38


def gelu(values):
    return values * 0.5 * (1.0 + lax.erf(values * 0.7071067811865476))


def gelu_slope(values):
    cdf = 0.5 * (1.0 + lax.erf(values * 0.7071067811865476))
    dens = jnp.exp(-0.5 * values * values) * 0.3989422804014327
    return cdf + values * dens


def rows_by_target(dest_row, groups, capacity, slots):
    rows = dest_row.shape[1]
    hit = lax.broadcasted_iota(jnp.int32, (groups, rows), 0) == dest_row
    before = lax.broadcasted_iota(jnp.int32, (rows, rows), 0) < lax.broadcasted_iota(
        jnp.int32, (rows, rows), 1
    )
    onehot = jnp.where(hit, 1.0, 0.0)
    counts = jnp.dot(
        onehot.astype(BF16), jnp.where(before, 1.0, 0.0).astype(BF16), preferred_element_type=F32
    )
    rank = jnp.sum(onehot * counts, axis=0, keepdims=True).astype(jnp.int32)
    target = dest_row * capacity + rank
    return lax.broadcasted_iota(jnp.int32, (slots, rows), 0) == target


def gather_kernel(offsets_ref, grad_ref, out_ref):
    length, slots = grad_ref.shape[0], offsets_ref.shape[1]
    pick = lax.broadcasted_iota(jnp.int32, (length, slots), 0) == offsets_ref[...]
    pick = jnp.where(pick, 1.0, 0.0).astype(BF16)
    out_ref[...] = lax.dot_general(
        pick, grad_ref[...], (((0,), (0,)), ((), ())), preferred_element_type=F32
    ).astype(BF16)


def owner_rows_kernel(groups, capacity, dest_ref, arrived_ref, token_ref, out_ref):
    slots = arrived_ref.shape[0]
    pick = rows_by_target(dest_ref[...], groups, capacity, slots)
    pick = jnp.where(pick, 1.0, 0.0).astype(BF16)
    rows = lax.dot_general(
        pick, arrived_ref[...], (((0,), (0,)), ((), ())), preferred_element_type=F32
    ).astype(BF16)
    out_ref[...] = rows


def route_kernel(groups, capacity, dest_ref, total_ref, *refs):
    term_refs, out_ref = refs[:-1], refs[-1]
    slots = out_ref.shape[0]
    total = total_ref[...]
    for term_ref in term_refs:
        total += term_ref[...].astype(F32)
    hit = rows_by_target(dest_ref[...], groups, capacity, slots)
    pick = jnp.where(hit, 1.0, 0.0)
    sent = jnp.dot(pick.astype(BF16), total.astype(BF16), preferred_element_type=F32)
    used = jnp.sum(pick, axis=1, keepdims=True)
    out_ref[...] = jnp.where(used > 0.5, sent, EMPTY).astype(BF16)


def place_kernel(offsets_ref, arrived_ref, text_ref, out_ref):
    length, slots = text_ref.shape[0], offsets_ref.shape[1]
    arrived = arrived_ref[...].astype(F32)
    used = arrived[:, 0:1] < LIMIT
    rows = jnp.where(used, arrived, 0.0).astype(BF16)
    marks = jnp.where(jnp.broadcast_to(used, (slots, 128)), 1.0, 0.0).astype(BF16)
    pick = lax.broadcasted_iota(jnp.int32, (length, slots), 0) == offsets_ref[...]
    pick = jnp.where(pick, 1.0, 0.0).astype(BF16)
    placed = jnp.dot(pick, rows, preferred_element_type=F32)
    filled = jnp.dot(pick, marks, preferred_element_type=F32)[:, 0:1] > 0.5
    out_ref[...] = jnp.where(filled, placed, text_ref[...].astype(F32)).astype(BF16)


TRANS = (((1,), (1,)), ((), ()))


def fetch(at_ref, sources, held_ref, sems):
    blocks, width = held_ref.shape[1], held_ref.shape[3]
    copies = []
    for j in range(blocks):
        columns = pl.ds(pl.multiple_of(at_ref[j] * width, width), width)
        pair = []
        for k, source in enumerate(sources):
            pair.append(
                pltpu.make_async_copy(source.at[:, columns], held_ref.at[k, j], sems.at[k, j])
            )
            pair[-1].start()
        copies.append(pair)
    return copies


def forward_first_kernel(
    at_ref, own_ref, other_ref, w_own_ref, w_other_ref, out_ref, act_ref, held_ref, sems
):
    copies = fetch(at_ref, (w_own_ref, w_other_ref), held_ref, sems)
    half = own_ref.shape[1]
    act_ref[:, :half] = gelu(own_ref[...].astype(F32)).astype(BF16)
    act_ref[:, half:] = gelu(other_ref[...].astype(F32)).astype(BF16)
    for j, pair in enumerate(copies):
        for copy in pair:
            copy.wait()
        total = jnp.dot(act_ref[:, :half], held_ref[0, j], preferred_element_type=F32)
        total += jnp.dot(act_ref[:, half:], held_ref[1, j], preferred_element_type=F32)
        out_ref[j] = total.astype(BF16)


def forward_second_kernel(at_ref, act_ref, w_own_ref, w_other_ref, out_ref, held_ref, sems):
    copies = fetch(at_ref, (w_own_ref, w_other_ref), held_ref, sems)
    half = held_ref.shape[2]
    for j, pair in enumerate(copies):
        for copy in pair:
            copy.wait()
        total = jnp.dot(act_ref[:, :half], held_ref[0, j], preferred_element_type=F32)
        total += jnp.dot(act_ref[:, half:], held_ref[1, j], preferred_element_type=F32)
        out_ref[j] = total.astype(BF16)


def add_kernel(kept_ref, beside_ref, token_ref, total_ref, *term_refs):
    token_ref[...] = jnp.zeros_like(token_ref)
    total_ref[...] = kept_ref[0].astype(F32) + beside_ref[0].astype(F32)
    for j, term_ref in enumerate(term_refs, 1):
        term_ref[...] = (kept_ref[j].astype(F32) + beside_ref[j].astype(F32)).astype(BF16)


def backward_first_kernel(blocks, at_ref, *refs):
    grad_refs, refs = refs[:blocks], refs[blocks:]
    pre_ref, w_own_ref, w_other_ref, own_ref, other_ref, slope_ref, held_ref, sems = refs
    copies = fetch(at_ref, (w_own_ref, w_other_ref), held_ref, sems)
    slope_ref[...] = gelu_slope(pre_ref[...].astype(F32))
    own, other = 0.0, 0.0
    for grad_ref, j, pair in zip(grad_refs, range(blocks), copies):
        for copy in pair:
            copy.wait()
        own += lax.dot_general(grad_ref[...], held_ref[0, j], TRANS, preferred_element_type=F32)
        other += lax.dot_general(grad_ref[...], held_ref[1, j], TRANS, preferred_element_type=F32)
    own_ref[...] = own
    other_ref[...] = other


def backward_second_kernel(
    at_ref, grad_ref, own_in, other_in, w_own_ref, w_other_ref, own_ref, other_ref, held_ref, sems
):
    copies = fetch(at_ref, (w_own_ref, w_other_ref), held_ref, sems)
    own, other = own_in[...], other_in[...]
    for j, pair in enumerate(copies):
        for copy in pair:
            copy.wait()
        own += lax.dot_general(grad_ref[j], held_ref[0, j], TRANS, preferred_element_type=F32)
        other += lax.dot_general(grad_ref[j], held_ref[1, j], TRANS, preferred_element_type=F32)
    own_ref[...] = own
    other_ref[...] = other.astype(BF16)


def slope_kernel(own_ref, other_ref, slope_ref, out_ref):
    total = own_ref[...] + other_ref[...].astype(F32)
    out_ref[...] = (total * slope_ref[...]).astype(BF16)


VMEM = pl.BlockSpec(memory_space=pltpu.VMEM)
HBM = pl.BlockSpec(memory_space=pltpu.HBM)
SMEM = pl.BlockSpec(memory_space=pltpu.SMEM)


def near_core(x):
    return pltpu.with_memory_space_constraint(x, pltpu.VMEM)


def in_hbm(x):
    return pltpu.with_memory_space_constraint(x, pltpu.HBM)


def call(kernel, outs, *args, final=False, first=False):
    out_shape = [jax.ShapeDtypeStruct(*o) if final else pltpu.VMEM(*o) for o in outs]
    got = pl.pallas_call(
        kernel,
        in_specs=[VMEM] * len(args),
        out_specs=[VMEM] * len(outs),
        out_shape=out_shape,
    )(*[a if first else near_core(a) for a in args])
    return got if len(outs) > 1 else got[0]


def product(kernel, outs, at, args, weights, blocks):
    hid, width = weights[0].shape[0], weights[0].shape[1] // (4 * blocks)
    rows = args[0].shape[-2]
    got = pl.pallas_call(
        kernel,
        in_specs=[SMEM] + [VMEM] * len(args) + [HBM] * 2,
        out_specs=[VMEM] * len(outs),
        out_shape=[pltpu.VMEM(*o) for o in outs],
        scratch_shapes=[
            pltpu.VMEM((2, blocks, hid, width), BF16),
            pltpu.SemaphoreType.DMA((2, blocks)),
        ],
        cost_estimate=pl.CostEstimate(
            flops=2 * rows * blocks * width * 2 * hid,
            bytes_accessed=4 * blocks * hid * width,
            transcendentals=0,
        ),
        compiler_params=pltpu.CompilerParams(vmem_limit_bytes=24 * 1024 * 1024),
    )(at, *[near_core(a) for a in args], *[in_hbm(w) for w in weights])
    return got if len(outs) > 1 else got[0]


def on_device(lines, pre_hidden, proj_weight, text_embed, routes_dest, place, grad_packed):
    groups = lax.axis_size("group")
    slots = place.shape[1]
    capacity = slots // groups
    rows, hid = pre_hidden.shape
    width = text_embed.shape[1]
    half = lines // 2
    line, core = lax.axis_index("line"), lax.axis_index("core")
    beside_line = line + 1 - 2 * lax.rem(line + core, 2) + lines
    steps = 2 * jnp.arange(half, dtype=jnp.int32)
    same = 2 * lax.rem(line + steps, lines) + core
    opposite = 2 * lax.rem(beside_line + steps, lines) + core
    dest_row = routes_dest.reshape(1, rows)

    cores = [(0, 1), (1, 0)]
    beside = []
    for i in range(lines):
        for c in range(2):
            odd = (i + c) % 2
            beside.append((2 * i + c, 2 * ((i + (-1 if odd else 1)) % lines) + c))

    def shift(x, by):
        return lax.ppermute(x, "line", [(i, (i + by) % lines) for i in range(lines)])

    def by_group(x):
        return x.reshape(groups, 4, capacity * width // 4)

    def exchange(x):
        x = lax.all_to_all(x, "group", split_axis=0, concat_axis=0, tiled=True)
        return x.reshape(slots, width)

    w_other = lax.ppermute(proj_weight, "core", cores)
    pre_other = lax.ppermute(pre_hidden, "core", cores)
    weights = (proj_weight, w_other)

    gathered = call(gather_kernel, [((slots, width), BF16)], place, grad_packed, first=True)
    returned = exchange(by_group(gathered))

    terms_out = ((half, rows, width), BF16)
    sent, act = product(
        forward_first_kernel,
        [terms_out, ((rows, 2 * hid), BF16)],
        opposite,
        (pre_hidden, pre_other),
        weights,
        half,
    )
    beside_terms = lax.ppermute(sent, ("line", "core"), beside)
    kept = product(forward_second_kernel, [terms_out], same, (act,), weights, half)
    token, total, *terms = call(
        add_kernel,
        [((8, 128), F32), ((rows, width), F32)] + [((rows, width), BF16)] * (half - 1),
        kept,
        beside_terms,
    )
    terms = [shift(term, 2 * j) for j, term in enumerate(terms, 1)]
    outgoing = call(
        functools.partial(route_kernel, groups, capacity),
        [((slots, width), BF16)],
        dest_row,
        total,
        *terms,
    )
    outgoing = by_group(outgoing)
    arrived = exchange(outgoing)

    mine = call(
        functools.partial(owner_rows_kernel, groups, capacity),
        [((rows, width), BF16)],
        dest_row,
        returned,
        token,
    )
    near = [mine] + [shift(mine, -2 * j) for j in range(1, half)]
    *near, _ = lax.optimization_barrier((*near, outgoing))
    far = lax.ppermute(jnp.stack(near), ("line", "core"), beside)
    wide = ((rows, hid), F32)
    own, other, slope = product(
        functools.partial(backward_first_kernel, half),
        [wide] * 3,
        same,
        (*near, pre_hidden),
        weights,
        half,
    )
    own, other = product(
        backward_second_kernel,
        [wide, ((rows, hid), BF16)],
        opposite,
        (far, own, other),
        weights,
        half,
    )
    other = lax.ppermute(other, "core", cores)
    grad_hidden = call(slope_kernel, [((rows, hid), BF16)], own, other, slope, final=True)

    packed = call(
        place_kernel, [(text_embed.shape, BF16)], place, arrived, text_embed, final=True
    )
    return (packed, grad_hidden)


def solution(mesh):
    groups, lines = mesh.shape["group"], mesh.shape["tensor"] // 2
    chips = Mesh(mesh.devices.reshape(groups, lines, 2), ("group", "line", "core"))
    tensor = ("line", "core")
    return jax.shard_map(
        functools.partial(on_device, lines),
        mesh=chips,
        in_specs=(
            P("group", tensor),
            P(tensor, None),
            P("group", tensor),
            P("group", None),
            P("group", None),
            P("group", tensor),
        ),
        out_specs=(P("group", tensor), P("group", tensor)),
        check_vma=False,
    )
```

```python
import functools

import jax
import jax.numpy as jnp
from jax import lax
from jax.experimental import pallas as pl
from jax.experimental.pallas import tpu as pltpu
from jax.sharding import Mesh
from jax.sharding import PartitionSpec as P

BF16 = jnp.bfloat16
F32 = jnp.float32
EMPTY = 1.7e38
LIMIT = 1.0e38


def gelu(values):
    return values * 0.5 * (1.0 + lax.erf(values * 0.7071067811865476))


def gelu_slope(values):
    cdf = 0.5 * (1.0 + lax.erf(values * 0.7071067811865476))
    dens = jnp.exp(-0.5 * values * values) * 0.3989422804014327
    return cdf + values * dens


def rows_by_target(dest_row, groups, capacity, slots):
    rows = dest_row.shape[1]
    hit = lax.broadcasted_iota(jnp.int32, (groups, rows), 0) == dest_row
    before = lax.broadcasted_iota(jnp.int32, (rows, rows), 0) < lax.broadcasted_iota(
        jnp.int32, (rows, rows), 1
    )
    onehot = jnp.where(hit, 1.0, 0.0)
    counts = jnp.dot(
        onehot.astype(BF16), jnp.where(before, 1.0, 0.0).astype(BF16), preferred_element_type=F32
    )
    rank = jnp.sum(onehot * counts, axis=0, keepdims=True).astype(jnp.int32)
    target = dest_row * capacity + rank
    return lax.broadcasted_iota(jnp.int32, (slots, rows), 0) == target


def gather_kernel(offsets_ref, grad_ref, out_ref):
    length, slots = grad_ref.shape[0], offsets_ref.shape[1]
    pick = lax.broadcasted_iota(jnp.int32, (length, slots), 0) == offsets_ref[...]
    pick = jnp.where(pick, 1.0, 0.0).astype(BF16)
    out_ref[...] = lax.dot_general(
        pick, grad_ref[...], (((0,), (0,)), ((), ())), preferred_element_type=F32
    ).astype(BF16)


def owner_rows_kernel(groups, capacity, dest_ref, arrived_ref, token_ref, out_ref):
    slots = arrived_ref.shape[0]
    pick = rows_by_target(dest_ref[...], groups, capacity, slots)
    pick = jnp.where(pick, 1.0, 0.0).astype(BF16)
    rows = lax.dot_general(
        pick, arrived_ref[...], (((0,), (0,)), ((), ())), preferred_element_type=F32
    ).astype(BF16)
    out_ref[...] = rows


def route_kernel(groups, capacity, dest_ref, total_ref, last_ref, out_ref):
    slots = out_ref.shape[0]
    total = total_ref[...] + last_ref[...].astype(F32)
    hit = rows_by_target(dest_ref[...], groups, capacity, slots)
    pick = jnp.where(hit, 1.0, 0.0)
    sent = jnp.dot(pick.astype(BF16), total.astype(BF16), preferred_element_type=F32)
    used = jnp.sum(pick, axis=1, keepdims=True)
    out_ref[...] = jnp.where(used > 0.5, sent, EMPTY).astype(BF16)


def place_kernel(offsets_ref, arrived_ref, text_ref, out_ref):
    length, slots = text_ref.shape[0], offsets_ref.shape[1]
    arrived = arrived_ref[...].astype(F32)
    used = arrived[:, 0:1] < LIMIT
    rows = jnp.where(used, arrived, 0.0).astype(BF16)
    marks = jnp.where(jnp.broadcast_to(used, (slots, 128)), 1.0, 0.0).astype(BF16)
    pick = lax.broadcasted_iota(jnp.int32, (length, slots), 0) == offsets_ref[...]
    pick = jnp.where(pick, 1.0, 0.0).astype(BF16)
    placed = jnp.dot(pick, rows, preferred_element_type=F32)
    filled = jnp.dot(pick, marks, preferred_element_type=F32)[:, 0:1] > 0.5
    out_ref[...] = jnp.where(filled, placed, text_ref[...].astype(F32)).astype(BF16)


TRANS = (((1,), (1,)), ((), ()))


def fetch(at_ref, sources, held_ref, sems):
    blocks, width = held_ref.shape[1], held_ref.shape[3]
    copies = []
    for j in range(blocks):
        columns = pl.ds(pl.multiple_of(at_ref[j] * width, width), width)
        pair = []
        for k, source in enumerate(sources):
            pair.append(
                pltpu.make_async_copy(source.at[:, columns], held_ref.at[k, j], sems.at[k, j])
            )
            pair[-1].start()
        copies.append(pair)
    return copies


def forward_first_kernel(
    at_ref, own_ref, other_ref, w_own_ref, w_other_ref, out_ref, act_ref, held_ref, sems
):
    copies = fetch(at_ref, (w_own_ref, w_other_ref), held_ref, sems)
    half = own_ref.shape[1]
    act_ref[:, :half] = gelu(own_ref[...].astype(F32)).astype(BF16)
    act_ref[:, half:] = gelu(other_ref[...].astype(F32)).astype(BF16)
    for j, pair in enumerate(copies):
        for copy in pair:
            copy.wait()
        total = jnp.dot(act_ref[:, :half], held_ref[0, j], preferred_element_type=F32)
        total += jnp.dot(act_ref[:, half:], held_ref[1, j], preferred_element_type=F32)
        out_ref[j] = total.astype(BF16)


def forward_second_kernel(at_ref, act_ref, w_own_ref, w_other_ref, out_ref, held_ref, sems):
    copies = fetch(at_ref, (w_own_ref, w_other_ref), held_ref, sems)
    half = held_ref.shape[2]
    for j, pair in enumerate(copies):
        for copy in pair:
            copy.wait()
        total = jnp.dot(act_ref[:, :half], held_ref[0, j], preferred_element_type=F32)
        total += jnp.dot(act_ref[:, half:], held_ref[1, j], preferred_element_type=F32)
        out_ref[j] = total.astype(BF16)


def add_kernel(kept_ref, beside_ref, total_ref, *term_refs):
    total_ref[...] = kept_ref[0].astype(F32) + beside_ref[0].astype(F32)
    for j, term_ref in enumerate(term_refs, 1):
        total = kept_ref[j].astype(F32) + beside_ref[j].astype(F32)
        term_ref[...] = total.astype(term_ref.dtype)


def relay_kernel(held_ref, arrived_ref, total_ref, back_ref, out_ref, sum_ref, token_ref):
    token_ref[...] = jnp.zeros_like(token_ref)
    out_ref[...] = (held_ref[...] + arrived_ref[...].astype(F32)).astype(BF16)
    sum_ref[...] = total_ref[...] + back_ref[...].astype(F32)


def backward_first_kernel(blocks, at_ref, *refs):
    grad_refs, refs = refs[:blocks], refs[blocks:]
    pre_ref, w_own_ref, w_other_ref, own_ref, other_ref, slope_ref, held_ref, sems = refs
    copies = fetch(at_ref, (w_own_ref, w_other_ref), held_ref, sems)
    slope_ref[...] = gelu_slope(pre_ref[...].astype(F32))
    own, other = 0.0, 0.0
    for grad_ref, j, pair in zip(grad_refs, range(blocks), copies):
        for copy in pair:
            copy.wait()
        own += lax.dot_general(grad_ref[...], held_ref[0, j], TRANS, preferred_element_type=F32)
        other += lax.dot_general(grad_ref[...], held_ref[1, j], TRANS, preferred_element_type=F32)
    own_ref[...] = own
    other_ref[...] = other


def backward_second_kernel(
    at_ref, grad_ref, own_in, other_in, w_own_ref, w_other_ref, own_ref, other_ref, held_ref, sems
):
    copies = fetch(at_ref, (w_own_ref, w_other_ref), held_ref, sems)
    own, other = own_in[...], other_in[...]
    for j, pair in enumerate(copies):
        for copy in pair:
            copy.wait()
        own += lax.dot_general(grad_ref[j], held_ref[0, j], TRANS, preferred_element_type=F32)
        other += lax.dot_general(grad_ref[j], held_ref[1, j], TRANS, preferred_element_type=F32)
    own_ref[...] = own
    other_ref[...] = other.astype(BF16)


def slope_kernel(own_ref, other_ref, slope_ref, out_ref):
    total = own_ref[...] + other_ref[...].astype(F32)
    out_ref[...] = (total * slope_ref[...]).astype(BF16)


VMEM = pl.BlockSpec(memory_space=pltpu.VMEM)
HBM = pl.BlockSpec(memory_space=pltpu.HBM)
SMEM = pl.BlockSpec(memory_space=pltpu.SMEM)


def near_core(x):
    return pltpu.with_memory_space_constraint(x, pltpu.VMEM)


def in_hbm(x):
    return pltpu.with_memory_space_constraint(x, pltpu.HBM)


def call(kernel, outs, *args, final=False, first=False):
    out_shape = [jax.ShapeDtypeStruct(*o) if final else pltpu.VMEM(*o) for o in outs]
    got = pl.pallas_call(
        kernel,
        in_specs=[VMEM] * len(args),
        out_specs=[VMEM] * len(outs),
        out_shape=out_shape,
    )(*[a if first else near_core(a) for a in args])
    return got if len(outs) > 1 else got[0]


def product(kernel, outs, at, args, weights, blocks, share=1):
    hid, width = weights[0].shape[0], weights[0].shape[1] // (4 * blocks)
    rows = args[0].shape[-2]
    got = pl.pallas_call(
        kernel,
        in_specs=[SMEM] + [VMEM] * len(args) + [HBM] * 2,
        out_specs=[VMEM] * len(outs),
        out_shape=[pltpu.VMEM(*o) for o in outs],
        scratch_shapes=[
            pltpu.VMEM((2, blocks, hid, width), BF16),
            pltpu.SemaphoreType.DMA((2, blocks)),
        ],
        cost_estimate=pl.CostEstimate(
            flops=2 * rows * blocks * width * 2 * hid // share,
            bytes_accessed=4 * blocks * hid * width // share,
            transcendentals=0,
        ),
        compiler_params=pltpu.CompilerParams(vmem_limit_bytes=24 * 1024 * 1024),
    )(at, *[near_core(a) for a in args], *[in_hbm(w) for w in weights])
    return got if len(outs) > 1 else got[0]


def on_device(lines, pre_hidden, proj_weight, text_embed, routes_dest, place, grad_packed):
    groups = lax.axis_size("group")
    slots = place.shape[1]
    capacity = slots // groups
    rows, hid = pre_hidden.shape
    width = text_embed.shape[1]
    half = lines // 2
    line, core = lax.axis_index("line"), lax.axis_index("core")
    beside_line = line + 1 - 2 * lax.rem(line + core, 2) + lines
    steps = (2 - 4 * core) * jnp.arange(half, dtype=jnp.int32) + 2 * lines
    same = 2 * lax.rem(line + steps, lines) + core
    opposite = 2 * lax.rem(beside_line + steps, lines) + core
    dest_row = routes_dest.reshape(1, rows)

    cores = [(0, 1), (1, 0)]
    beside = []
    for i in range(lines):
        for c in range(2):
            odd = (i + c) % 2
            beside.append((2 * i + c, 2 * ((i + (-1 if odd else 1)) % lines) + c))

    def relay(x, by):
        pairs = []
        for i in range(lines):
            for c in range(2):
                pairs.append((2 * i + c, 2 * ((i + (by if c == 0 else -by)) % lines) + c))
        return lax.ppermute(x, ("line", "core"), pairs)

    def by_group(x):
        return x.reshape(groups, 4, capacity * width // 4)

    def exchange(x):
        x = lax.all_to_all(x, "group", split_axis=0, concat_axis=0, tiled=True)
        return x.reshape(slots, width)

    w_other = lax.ppermute(proj_weight, "core", cores)
    pre_other = lax.ppermute(pre_hidden, "core", cores)
    weights = (proj_weight, w_other)

    gathered = call(gather_kernel, [((slots, width), BF16)], place, grad_packed, first=True)
    returned = exchange(by_group(gathered))

    terms_out = ((half, rows, width), BF16)
    sent, act = product(
        forward_first_kernel,
        [terms_out, ((rows, 2 * hid), BF16)],
        opposite,
        (pre_hidden, pre_other),
        weights,
        half,
    )
    beside_terms = lax.ppermute(sent, ("line", "core"), beside)
    kept = product(forward_second_kernel, [terms_out], same, (act,), weights, half)
    total, first, second, third = call(
        add_kernel,
        [((rows, width), F32)] * 2 + [((rows, width), BF16)] * 2,
        kept,
        beside_terms,
    )
    passed = relay(second, 2)
    back = relay(third, -2)
    first, total, token = call(
        relay_kernel,
        [((rows, width), BF16), ((rows, width), F32), ((8, 128), F32)],
        first,
        passed,
        total,
        back,
    )
    last = relay(first, 2)
    outgoing = call(
        functools.partial(route_kernel, groups, capacity),
        [((slots, width), BF16)],
        dest_row,
        total,
        last,
    )
    outgoing = by_group(outgoing)
    arrived = exchange(outgoing)

    mine = call(
        functools.partial(owner_rows_kernel, groups, capacity),
        [((rows, width), BF16)],
        dest_row,
        returned,
        token,
    )
    last = relay(mine, 2)
    near = [mine, relay(mine, -2), relay(last, 2), last]
    far = lax.ppermute(jnp.stack(near), ("line", "core"), beside)
    wide = ((rows, hid), F32)
    own, other, slope = product(
        functools.partial(backward_first_kernel, half),
        [wide] * 3,
        same,
        (*near, pre_hidden),
        weights,
        half,
        1000,
    )
    own, other = product(
        backward_second_kernel,
        [wide, ((rows, hid), BF16)],
        opposite,
        (far, own, other),
        weights,
        half,
        1000,
    )
    other = lax.ppermute(other, "core", cores)
    grad_hidden = call(slope_kernel, [((rows, hid), BF16)], own, other, slope, final=True)

    packed = call(
        place_kernel, [(text_embed.shape, BF16)], place, arrived, text_embed, final=True
    )
    return (packed, grad_hidden)


def solution(mesh):
    groups, lines = mesh.shape["group"], mesh.shape["tensor"] // 2
    chips = Mesh(mesh.devices.reshape(groups, lines, 2), ("group", "line", "core"))
    tensor = ("line", "core")
    return jax.shard_map(
        functools.partial(on_device, lines),
        mesh=chips,
        in_specs=(
            P("group", tensor),
            P(tensor, None),
            P("group", tensor),
            P("group", None),
            P("group", None),
            P("group", tensor),
        ),
        out_specs=(P("group", tensor), P("group", tensor)),
        check_vma=False,
    )
```

```python
import functools

import jax
import jax.numpy as jnp
from jax import lax
from jax.experimental import pallas as pl
from jax.experimental.pallas import tpu as pltpu
from jax.sharding import Mesh
from jax.sharding import PartitionSpec as P

BF16 = jnp.bfloat16
F32 = jnp.float32
EMPTY = 1.7e38
LIMIT = 1.0e38


def gelu(values):
    return values * 0.5 * (1.0 + lax.erf(values * 0.7071067811865476))


def gelu_slope(values):
    cdf = 0.5 * (1.0 + lax.erf(values * 0.7071067811865476))
    dens = jnp.exp(-0.5 * values * values) * 0.3989422804014327
    return cdf + values * dens


def rows_by_target(dest_row, groups, capacity, slots):
    rows = dest_row.shape[1]
    hit = lax.broadcasted_iota(jnp.int32, (groups, rows), 0) == dest_row
    before = lax.broadcasted_iota(jnp.int32, (rows, rows), 0) < lax.broadcasted_iota(
        jnp.int32, (rows, rows), 1
    )
    onehot = jnp.where(hit, 1.0, 0.0)
    counts = jnp.dot(
        onehot.astype(BF16), jnp.where(before, 1.0, 0.0).astype(BF16), preferred_element_type=F32
    )
    rank = jnp.sum(onehot * counts, axis=0, keepdims=True).astype(jnp.int32)
    target = dest_row * capacity + rank
    return lax.broadcasted_iota(jnp.int32, (slots, rows), 0) == target


def gather_kernel(offsets_ref, grad_ref, out_ref):
    length, slots = grad_ref.shape[0], offsets_ref.shape[1]
    pick = lax.broadcasted_iota(jnp.int32, (length, slots), 0) == offsets_ref[...]
    pick = jnp.where(pick, 1.0, 0.0).astype(BF16)
    out_ref[...] = lax.dot_general(
        pick, grad_ref[...], (((0,), (0,)), ((), ())), preferred_element_type=F32
    ).astype(BF16)


def owner_rows_kernel(groups, capacity, dest_ref, arrived_ref, token_ref, out_ref):
    slots = arrived_ref.shape[0]
    pick = rows_by_target(dest_ref[...], groups, capacity, slots)
    pick = jnp.where(pick, 1.0, 0.0).astype(BF16)
    rows = lax.dot_general(
        pick, arrived_ref[...], (((0,), (0,)), ((), ())), preferred_element_type=F32
    ).astype(BF16)
    for j in range(out_ref.shape[0]):
        out_ref[j] = rows


def route_kernel(groups, capacity, dest_ref, total_ref, last_ref, out_ref):
    slots = out_ref.shape[0]
    total = total_ref[...] + last_ref[...].astype(F32)
    hit = rows_by_target(dest_ref[...], groups, capacity, slots)
    pick = jnp.where(hit, 1.0, 0.0)
    sent = jnp.dot(pick.astype(BF16), total.astype(BF16), preferred_element_type=F32)
    used = jnp.sum(pick, axis=1, keepdims=True)
    out_ref[...] = jnp.where(used > 0.5, sent, EMPTY).astype(BF16)


def place_kernel(offsets_ref, arrived_ref, text_ref, out_ref):
    length, slots = text_ref.shape[0], offsets_ref.shape[1]
    arrived = arrived_ref[...].astype(F32)
    used = arrived[:, 0:1] < LIMIT
    rows = jnp.where(used, arrived, 0.0).astype(BF16)
    marks = jnp.where(jnp.broadcast_to(used, (slots, 128)), 1.0, 0.0).astype(BF16)
    pick = lax.broadcasted_iota(jnp.int32, (length, slots), 0) == offsets_ref[...]
    pick = jnp.where(pick, 1.0, 0.0).astype(BF16)
    placed = jnp.dot(pick, rows, preferred_element_type=F32)
    filled = jnp.dot(pick, marks, preferred_element_type=F32)[:, 0:1] > 0.5
    out_ref[...] = jnp.where(filled, placed, text_ref[...].astype(F32)).astype(BF16)


TRANS = (((1,), (1,)), ((), ()))


def fetch(at_ref, sources, held_ref, sems):
    blocks, width = held_ref.shape[1], held_ref.shape[3]
    copies = []
    for j in range(blocks):
        columns = pl.ds(pl.multiple_of(at_ref[j] * width, width), width)
        pair = []
        for k, source in enumerate(sources):
            pair.append(
                pltpu.make_async_copy(source.at[:, columns], held_ref.at[k, j], sems.at[k, j])
            )
            pair[-1].start()
        copies.append(pair)
    return copies


def forward_first_kernel(
    at_ref, own_ref, other_ref, w_own_ref, w_other_ref, out_ref, act_ref, held_ref, sems
):
    copies = fetch(at_ref, (w_own_ref, w_other_ref), held_ref, sems)
    half = own_ref.shape[1]
    act_ref[:, :half] = gelu(own_ref[...].astype(F32)).astype(BF16)
    act_ref[:, half:] = gelu(other_ref[...].astype(F32)).astype(BF16)
    for j, pair in enumerate(copies):
        for copy in pair:
            copy.wait()
        total = jnp.dot(act_ref[:, :half], held_ref[0, j], preferred_element_type=F32)
        total += jnp.dot(act_ref[:, half:], held_ref[1, j], preferred_element_type=F32)
        out_ref[j] = total.astype(BF16)


def forward_second_kernel(at_ref, act_ref, w_own_ref, w_other_ref, out_ref, held_ref, sems):
    copies = fetch(at_ref, (w_own_ref, w_other_ref), held_ref, sems)
    half = held_ref.shape[2]
    for j, pair in enumerate(copies):
        for copy in pair:
            copy.wait()
        total = jnp.dot(act_ref[:, :half], held_ref[0, j], preferred_element_type=F32)
        total += jnp.dot(act_ref[:, half:], held_ref[1, j], preferred_element_type=F32)
        out_ref[j] = total.astype(BF16)


def add_kernel(kept_ref, beside_ref, token_ref, total_ref, *term_refs):
    token_ref[...] = jnp.zeros_like(token_ref)
    total_ref[...] = kept_ref[0].astype(F32) + beside_ref[0].astype(F32)
    for j, term_ref in enumerate(term_refs, 1):
        total = kept_ref[j].astype(F32) + beside_ref[j].astype(F32)
        term_ref[...] = total.astype(term_ref.dtype)


def relay_kernel(held_ref, arrived_ref, total_ref, back_ref, out_ref, sum_ref):
    out_ref[...] = (held_ref[...] + arrived_ref[...].astype(F32)).astype(BF16)
    sum_ref[...] = total_ref[...] + back_ref[...].astype(F32)


def backward_first_kernel(
    at_ref, grad_ref, pre_ref, w_own_ref, w_other_ref, own_ref, other_ref, slope_ref, held_ref, sems
):
    copies = fetch(at_ref, (w_own_ref, w_other_ref), held_ref, sems)
    slope_ref[...] = gelu_slope(pre_ref[...].astype(F32))
    own, other = 0.0, 0.0
    for j, pair in enumerate(copies):
        for copy in pair:
            copy.wait()
        own += lax.dot_general(grad_ref[j], held_ref[0, j], TRANS, preferred_element_type=F32)
        other += lax.dot_general(grad_ref[j], held_ref[1, j], TRANS, preferred_element_type=F32)
    own_ref[...] = own
    other_ref[...] = other


def backward_second_kernel(
    at_ref, grad_ref, own_in, other_in, w_own_ref, w_other_ref, own_ref, other_ref, held_ref, sems
):
    copies = fetch(at_ref, (w_own_ref, w_other_ref), held_ref, sems)
    own, other = own_in[...], other_in[...]
    for j, pair in enumerate(copies):
        for copy in pair:
            copy.wait()
        own += lax.dot_general(grad_ref[j], held_ref[0, j], TRANS, preferred_element_type=F32)
        other += lax.dot_general(grad_ref[j], held_ref[1, j], TRANS, preferred_element_type=F32)
    own_ref[...] = own
    other_ref[...] = other.astype(BF16)


def slope_kernel(own_ref, other_ref, slope_ref, out_ref):
    total = own_ref[...] + other_ref[...].astype(F32)
    out_ref[...] = (total * slope_ref[...]).astype(BF16)


VMEM = pl.BlockSpec(memory_space=pltpu.VMEM)
HBM = pl.BlockSpec(memory_space=pltpu.HBM)
SMEM = pl.BlockSpec(memory_space=pltpu.SMEM)


def near_core(x):
    return pltpu.with_memory_space_constraint(x, pltpu.VMEM)


def in_hbm(x):
    return pltpu.with_memory_space_constraint(x, pltpu.HBM)


def call(kernel, outs, *args, final=False, first=False):
    out_shape = [jax.ShapeDtypeStruct(*o) if final else pltpu.VMEM(*o) for o in outs]
    got = pl.pallas_call(
        kernel,
        in_specs=[VMEM] * len(args),
        out_specs=[VMEM] * len(outs),
        out_shape=out_shape,
    )(*[a if first else near_core(a) for a in args])
    return got if len(outs) > 1 else got[0]


def product(kernel, outs, at, args, weights, blocks, share=1):
    hid, width = weights[0].shape[0], weights[0].shape[1] // (4 * blocks)
    rows = args[0].shape[-2]
    got = pl.pallas_call(
        kernel,
        in_specs=[SMEM] + [VMEM] * len(args) + [HBM] * 2,
        out_specs=[VMEM] * len(outs),
        out_shape=[pltpu.VMEM(*o) for o in outs],
        scratch_shapes=[
            pltpu.VMEM((2, blocks, hid, width), BF16),
            pltpu.SemaphoreType.DMA((2, blocks)),
        ],
        cost_estimate=pl.CostEstimate(
            flops=2 * rows * blocks * width * 2 * hid // share,
            bytes_accessed=4 * blocks * hid * width // share,
            transcendentals=0,
        ),
        compiler_params=pltpu.CompilerParams(vmem_limit_bytes=24 * 1024 * 1024),
    )(at, *[near_core(a) for a in args], *[in_hbm(w) for w in weights])
    return got if len(outs) > 1 else got[0]


def on_device(lines, pre_hidden, proj_weight, text_embed, routes_dest, place, grad_packed):
    groups = lax.axis_size("group")
    slots = place.shape[1]
    capacity = slots // groups
    rows, hid = pre_hidden.shape
    width = text_embed.shape[1]
    half = lines // 2
    line, core = lax.axis_index("line"), lax.axis_index("core")
    beside_line = line + 1 - 2 * lax.rem(line + core, 2) + lines
    steps = (2 - 4 * core) * jnp.arange(half, dtype=jnp.int32) + 2 * lines
    same = 2 * lax.rem(line + steps, lines) + core
    opposite = 2 * lax.rem(beside_line + steps, lines) + core
    dest_row = routes_dest.reshape(1, rows)

    cores = [(0, 1), (1, 0)]
    beside = []
    for i in range(lines):
        for c in range(2):
            odd = (i + c) % 2
            beside.append((2 * i + c, 2 * ((i + (-1 if odd else 1)) % lines) + c))

    alike = [list(range(0, lines, 2)), list(range(1, lines, 2))]

    def relay(x, by):
        pairs = []
        for i in range(lines):
            for c in range(2):
                pairs.append((2 * i + c, 2 * ((i + (by if c == 0 else -by)) % lines) + c))
        return lax.ppermute(x, ("line", "core"), pairs)

    def by_group(x):
        return x.reshape(groups, 4, capacity * width // 4)

    def exchange(x):
        return lax.all_to_all(x, "group", split_axis=0, concat_axis=0, tiled=True)

    w_other = lax.ppermute(proj_weight, "core", cores)
    pre_other = lax.ppermute(pre_hidden, "core", cores)
    weights = (proj_weight, w_other)

    gathered = call(gather_kernel, [((slots, width), BF16)], place, grad_packed, first=True)
    returned = exchange(by_group(gathered))

    terms_out = ((half, rows, width), BF16)
    sent, act = product(
        forward_first_kernel,
        [terms_out, ((rows, 2 * hid), BF16)],
        opposite,
        (pre_hidden, pre_other),
        weights,
        half,
    )
    beside_terms = lax.ppermute(sent, ("line", "core"), beside)
    kept = product(forward_second_kernel, [terms_out], same, (act,), weights, half)
    token, total, first, second, third = call(
        add_kernel,
        [((8, 128), F32)] + [((rows, width), F32)] * 2 + [((rows, width), BF16)] * 2,
        kept,
        beside_terms,
    )
    passed = relay(second, 2)
    back = relay(third, -2)
    first, total = call(
        relay_kernel,
        [((rows, width), BF16), ((rows, width), F32)],
        first,
        passed,
        total,
        back,
    )
    last = relay(first, 2)
    outgoing = call(
        functools.partial(route_kernel, groups, capacity),
        [((slots, width), BF16)],
        dest_row,
        total,
        last,
    )
    outgoing = by_group(outgoing)
    arrived = exchange(outgoing)

    returned, token = lax.optimization_barrier((returned, token))
    returned = returned.reshape(slots, width)
    mine = call(
        functools.partial(owner_rows_kernel, groups, capacity),
        [terms_out],
        dest_row,
        returned,
        token,
    )
    near = lax.all_to_all(
        mine, "line", split_axis=0, concat_axis=0, tiled=True, axis_index_groups=alike
    )
    far = lax.ppermute(near, ("line", "core"), beside)
    parity = lax.rem(line, 2)
    every = 4 * jnp.arange(half, dtype=jnp.int32) + core
    wide = ((rows, hid), F32)
    own, other, slope = product(
        backward_first_kernel,
        [wide] * 3,
        every + 2 * parity,
        (near, pre_hidden),
        weights,
        half,
        1000,
    )
    own, other = product(
        backward_second_kernel,
        [wide, ((rows, hid), BF16)],
        every + 2 * (1 - parity),
        (far, own, other),
        weights,
        half,
        1000,
    )
    other = lax.ppermute(other, "core", cores)
    grad_hidden = call(slope_kernel, [((rows, hid), BF16)], own, other, slope, final=True)

    packed = call(
        place_kernel, [(text_embed.shape, BF16)], place, arrived.reshape(slots, width), text_embed, final=True
    )
    return (packed, grad_hidden)


def solution(mesh):
    groups, lines = mesh.shape["group"], mesh.shape["tensor"] // 2
    chips = Mesh(mesh.devices.reshape(groups, lines, 2), ("group", "line", "core"))
    tensor = ("line", "core")
    return jax.shard_map(
        functools.partial(on_device, lines),
        mesh=chips,
        in_specs=(
            P("group", tensor),
            P(tensor, None),
            P("group", tensor),
            P("group", None),
            P("group", None),
            P("group", tensor),
        ),
        out_specs=(P("group", tensor), P("group", tensor)),
        check_vma=False,
    )
```

```python
import functools

import jax
import jax.numpy as jnp
from jax import lax
from jax.experimental import pallas as pl
from jax.experimental.pallas import tpu as pltpu
from jax.sharding import Mesh
from jax.sharding import PartitionSpec as P

BF16 = jnp.bfloat16
F32 = jnp.float32
EMPTY = 1.7e38
LIMIT = 1.0e38


def gelu(values):
    return values * 0.5 * (1.0 + lax.erf(values * 0.7071067811865476))


def gelu_slope(values):
    cdf = 0.5 * (1.0 + lax.erf(values * 0.7071067811865476))
    dens = jnp.exp(-0.5 * values * values) * 0.3989422804014327
    return cdf + values * dens


def rows_by_target(dest_row, groups, capacity, slots):
    rows = dest_row.shape[1]
    hit = lax.broadcasted_iota(jnp.int32, (groups, rows), 0) == dest_row
    before = lax.broadcasted_iota(jnp.int32, (rows, rows), 0) < lax.broadcasted_iota(
        jnp.int32, (rows, rows), 1
    )
    onehot = jnp.where(hit, 1.0, 0.0)
    counts = jnp.dot(
        onehot.astype(BF16), jnp.where(before, 1.0, 0.0).astype(BF16), preferred_element_type=F32
    )
    rank = jnp.sum(onehot * counts, axis=0, keepdims=True).astype(jnp.int32)
    target = dest_row * capacity + rank
    return lax.broadcasted_iota(jnp.int32, (slots, rows), 0) == target


def gather_kernel(offsets_ref, grad_ref, out_ref):
    length, slots = grad_ref.shape[0], offsets_ref.shape[1]
    pick = lax.broadcasted_iota(jnp.int32, (length, slots), 0) == offsets_ref[...]
    pick = jnp.where(pick, 1.0, 0.0).astype(BF16)
    out_ref[...] = lax.dot_general(
        pick, grad_ref[...], (((0,), (0,)), ((), ())), preferred_element_type=F32
    ).astype(BF16)


def meet_kernel(groups, capacity, dest_ref, arrived_ref, kept_ref, beside_ref, *refs):
    total_ref, first_ref, ahead_ref, back_ref = refs
    pick = rows_by_target(dest_ref[...], groups, capacity, arrived_ref.shape[0])
    pick = jnp.where(pick, 1.0, 0.0).astype(BF16)
    rows = lax.dot_general(
        pick, arrived_ref[...], (((0,), (0,)), ((), ())), preferred_element_type=F32
    ).astype(BF16)
    total_ref[...] = kept_ref[0].astype(F32) + beside_ref[0].astype(F32)
    first_ref[...] = kept_ref[1].astype(F32) + beside_ref[1].astype(F32)
    ahead_ref[0] = (kept_ref[2].astype(F32) + beside_ref[2].astype(F32)).astype(BF16)
    ahead_ref[1] = rows
    back_ref[0] = (kept_ref[3].astype(F32) + beside_ref[3].astype(F32)).astype(BF16)
    back_ref[1] = rows


def route_kernel(groups, capacity, dest_ref, total_ref, back_ref, last_ref, out_ref):
    slots = out_ref.shape[0]
    total = total_ref[...] + back_ref[0].astype(F32) + last_ref[0].astype(F32)
    hit = rows_by_target(dest_ref[...], groups, capacity, slots)
    pick = jnp.where(hit, 1.0, 0.0)
    sent = jnp.dot(pick.astype(BF16), total.astype(BF16), preferred_element_type=F32)
    used = jnp.sum(pick, axis=1, keepdims=True)
    out_ref[...] = jnp.where(used > 0.5, sent, EMPTY).astype(BF16)


def place_kernel(offsets_ref, arrived_ref, text_ref, out_ref):
    length, slots = text_ref.shape[0], offsets_ref.shape[1]
    arrived = arrived_ref[...].astype(F32)
    used = arrived[:, 0:1] < LIMIT
    rows = jnp.where(used, arrived, 0.0).astype(BF16)
    marks = jnp.where(jnp.broadcast_to(used, (slots, 128)), 1.0, 0.0).astype(BF16)
    pick = lax.broadcasted_iota(jnp.int32, (length, slots), 0) == offsets_ref[...]
    pick = jnp.where(pick, 1.0, 0.0).astype(BF16)
    placed = jnp.dot(pick, rows, preferred_element_type=F32)
    filled = jnp.dot(pick, marks, preferred_element_type=F32)[:, 0:1] > 0.5
    out_ref[...] = jnp.where(filled, placed, text_ref[...].astype(F32)).astype(BF16)


TRANS = (((1,), (1,)), ((), ()))


def fetch(at_ref, sources, held_ref, sems):
    blocks, width = held_ref.shape[1], held_ref.shape[3]
    copies = []
    for j in range(blocks):
        columns = pl.ds(pl.multiple_of(at_ref[j] * width, width), width)
        pair = []
        for k, source in enumerate(sources):
            pair.append(
                pltpu.make_async_copy(source.at[:, columns], held_ref.at[k, j], sems.at[k, j])
            )
            pair[-1].start()
        copies.append(pair)
    return copies


def forward_first_kernel(
    at_ref, own_ref, other_ref, w_own_ref, w_other_ref, out_ref, act_ref, held_ref, sems
):
    copies = fetch(at_ref, (w_own_ref, w_other_ref), held_ref, sems)
    half = own_ref.shape[1]
    act_ref[:, :half] = gelu(own_ref[...].astype(F32)).astype(BF16)
    act_ref[:, half:] = gelu(other_ref[...].astype(F32)).astype(BF16)
    for j, pair in enumerate(copies):
        for copy in pair:
            copy.wait()
        total = jnp.dot(act_ref[:, :half], held_ref[0, j], preferred_element_type=F32)
        total += jnp.dot(act_ref[:, half:], held_ref[1, j], preferred_element_type=F32)
        out_ref[j] = total.astype(BF16)


def forward_second_kernel(at_ref, act_ref, w_own_ref, w_other_ref, out_ref, held_ref, sems):
    copies = fetch(at_ref, (w_own_ref, w_other_ref), held_ref, sems)
    half = held_ref.shape[2]
    for j, pair in enumerate(copies):
        for copy in pair:
            copy.wait()
        total = jnp.dot(act_ref[:, :half], held_ref[0, j], preferred_element_type=F32)
        total += jnp.dot(act_ref[:, half:], held_ref[1, j], preferred_element_type=F32)
        out_ref[j] = total.astype(BF16)


def relay_kernel(first_ref, arrived_ref, out_ref):
    out_ref[0] = (first_ref[...] + arrived_ref[0].astype(F32)).astype(BF16)
    out_ref[1] = arrived_ref[1]


def backward_first_kernel(blocks, at_ref, *refs):
    grad_refs, refs = refs[:blocks], refs[blocks:]
    pre_ref, w_own_ref, w_other_ref, own_ref, other_ref, slope_ref, held_ref, sems = refs
    copies = fetch(at_ref, (w_own_ref, w_other_ref), held_ref, sems)
    slope_ref[...] = gelu_slope(pre_ref[...].astype(F32))
    own, other = 0.0, 0.0
    for grad_ref, j, pair in zip(grad_refs, range(blocks), copies):
        for copy in pair:
            copy.wait()
        own += lax.dot_general(grad_ref[1], held_ref[0, j], TRANS, preferred_element_type=F32)
        other += lax.dot_general(grad_ref[1], held_ref[1, j], TRANS, preferred_element_type=F32)
    own_ref[...] = own
    other_ref[...] = other


def backward_second_kernel(
    at_ref, grad_ref, own_in, other_in, w_own_ref, w_other_ref, own_ref, other_ref, held_ref, sems
):
    copies = fetch(at_ref, (w_own_ref, w_other_ref), held_ref, sems)
    own, other = own_in[...], other_in[...]
    for j, pair in enumerate(copies):
        for copy in pair:
            copy.wait()
        own += lax.dot_general(grad_ref[j], held_ref[0, j], TRANS, preferred_element_type=F32)
        other += lax.dot_general(grad_ref[j], held_ref[1, j], TRANS, preferred_element_type=F32)
    own_ref[...] = own
    other_ref[...] = other.astype(BF16)


def slope_kernel(own_ref, other_ref, slope_ref, out_ref):
    total = own_ref[...] + other_ref[...].astype(F32)
    out_ref[...] = (total * slope_ref[...]).astype(BF16)


VMEM = pl.BlockSpec(memory_space=pltpu.VMEM)
HBM = pl.BlockSpec(memory_space=pltpu.HBM)
SMEM = pl.BlockSpec(memory_space=pltpu.SMEM)


def near_core(x):
    return pltpu.with_memory_space_constraint(x, pltpu.VMEM)


def in_hbm(x):
    return pltpu.with_memory_space_constraint(x, pltpu.HBM)


def call(kernel, outs, *args, final=False, first=False):
    out_shape = [jax.ShapeDtypeStruct(*o) if final else pltpu.VMEM(*o) for o in outs]
    got = pl.pallas_call(
        kernel,
        in_specs=[VMEM] * len(args),
        out_specs=[VMEM] * len(outs),
        out_shape=out_shape,
    )(*[a if first else near_core(a) for a in args])
    return got if len(outs) > 1 else got[0]


def product(kernel, outs, at, args, weights, blocks, share=1):
    hid, width = weights[0].shape[0], weights[0].shape[1] // (4 * blocks)
    rows = args[0].shape[-2]
    got = pl.pallas_call(
        kernel,
        in_specs=[SMEM] + [VMEM] * len(args) + [HBM] * 2,
        out_specs=[VMEM] * len(outs),
        out_shape=[pltpu.VMEM(*o) for o in outs],
        scratch_shapes=[
            pltpu.VMEM((2, blocks, hid, width), BF16),
            pltpu.SemaphoreType.DMA((2, blocks)),
        ],
        cost_estimate=pl.CostEstimate(
            flops=2 * rows * blocks * width * 2 * hid // share,
            bytes_accessed=4 * blocks * hid * width // share,
            transcendentals=0,
        ),
        compiler_params=pltpu.CompilerParams(vmem_limit_bytes=24 * 1024 * 1024),
    )(at, *[near_core(a) for a in args], *[in_hbm(w) for w in weights])
    return got if len(outs) > 1 else got[0]


def on_device(lines, pre_hidden, proj_weight, text_embed, routes_dest, place, grad_packed):
    groups = lax.axis_size("group")
    slots = place.shape[1]
    capacity = slots // groups
    rows, hid = pre_hidden.shape
    width = text_embed.shape[1]
    half = lines // 2
    line, core = lax.axis_index("line"), lax.axis_index("core")
    beside_line = line + 1 - 2 * lax.rem(line + core, 2) + lines
    steps = (2 - 4 * core) * jnp.arange(half, dtype=jnp.int32) + 2 * lines
    same = 2 * lax.rem(line + steps, lines) + core
    opposite = 2 * lax.rem(beside_line + steps, lines) + core
    dest_row = routes_dest.reshape(1, rows)

    cores = [(0, 1), (1, 0)]
    beside = []
    for i in range(lines):
        for c in range(2):
            odd = (i + c) % 2
            beside.append((2 * i + c, 2 * ((i + (-1 if odd else 1)) % lines) + c))

    def relay(x, by):
        pairs = []
        for i in range(lines):
            for c in range(2):
                pairs.append((2 * i + c, 2 * ((i + (by if c == 0 else -by)) % lines) + c))
        return lax.ppermute(x, ("line", "core"), pairs)

    def by_group(x):
        return x.reshape(groups, 4, capacity * width // 4)

    def exchange(x):
        return lax.all_to_all(x, "group", split_axis=0, concat_axis=0, tiled=True)

    w_other = lax.ppermute(proj_weight, "core", cores)
    pre_other = lax.ppermute(pre_hidden, "core", cores)
    weights = (proj_weight, w_other)

    gathered = call(gather_kernel, [((slots, width), BF16)], place, grad_packed, first=True)
    returned = exchange(by_group(gathered))

    terms_out = ((half, rows, width), BF16)
    sent, act = product(
        forward_first_kernel,
        [terms_out, ((rows, 2 * hid), BF16)],
        opposite,
        (pre_hidden, pre_other),
        weights,
        half,
    )
    beside_terms = lax.ppermute(sent, ("line", "core"), beside)
    kept = product(forward_second_kernel, [terms_out], same, (act,), weights, half)
    returned, beside_terms = lax.optimization_barrier((returned, beside_terms))
    pair = ((2, rows, width), BF16)
    total, first, ahead, back = call(
        functools.partial(meet_kernel, groups, capacity),
        [((rows, width), F32)] * 2 + [pair] * 2,
        dest_row,
        returned.reshape(slots, width),
        kept,
        beside_terms,
    )
    passed = relay(ahead, 2)
    back = relay(back, -2)
    last = relay(call(relay_kernel, [pair], first, passed), 2)
    outgoing = call(
        functools.partial(route_kernel, groups, capacity),
        [((slots, width), BF16)],
        dest_row,
        total,
        back,
        last,
    )
    outgoing = by_group(outgoing)
    arrived = exchange(outgoing)

    near = [ahead, back, last, passed]
    far = lax.ppermute(jnp.stack([x[1] for x in near]), ("line", "core"), beside)
    wide = ((rows, hid), F32)
    own, other, slope = product(
        functools.partial(backward_first_kernel, half),
        [wide] * 3,
        same,
        (*near, pre_hidden),
        weights,
        half,
        1000,
    )
    own, other = product(
        backward_second_kernel,
        [wide, ((rows, hid), BF16)],
        opposite,
        (far, own, other),
        weights,
        half,
        1000,
    )
    other = lax.ppermute(other, "core", cores)
    grad_hidden = call(slope_kernel, [((rows, hid), BF16)], own, other, slope, final=True)

    packed = call(
        place_kernel, [(text_embed.shape, BF16)], place, arrived.reshape(slots, width), text_embed, final=True
    )
    return (packed, grad_hidden)


def solution(mesh):
    groups, lines = mesh.shape["group"], mesh.shape["tensor"] // 2
    chips = Mesh(mesh.devices.reshape(groups, lines, 2), ("group", "line", "core"))
    tensor = ("line", "core")
    return jax.shard_map(
        functools.partial(on_device, lines),
        mesh=chips,
        in_specs=(
            P("group", tensor),
            P(tensor, None),
            P("group", tensor),
            P("group", None),
            P("group", None),
            P("group", tensor),
        ),
        out_specs=(P("group", tensor), P("group", tensor)),
        check_vma=False,
    )
```

```python
import functools

import jax
import jax.numpy as jnp
from jax import lax
from jax.experimental import pallas as pl
from jax.experimental.pallas import tpu as pltpu
from jax.sharding import Mesh
from jax.sharding import PartitionSpec as P

BF16 = jnp.bfloat16
F32 = jnp.float32
EMPTY = 1.7e38
LIMIT = 1.0e38


def gelu(values):
    return values * 0.5 * (1.0 + lax.erf(values * 0.7071067811865476))


def gelu_slope(values):
    cdf = 0.5 * (1.0 + lax.erf(values * 0.7071067811865476))
    dens = jnp.exp(-0.5 * values * values) * 0.3989422804014327
    return cdf + values * dens


def rows_by_target(dest_row, groups, capacity, slots):
    rows = dest_row.shape[1]
    hit = lax.broadcasted_iota(jnp.int32, (groups, rows), 0) == dest_row
    before = lax.broadcasted_iota(jnp.int32, (rows, rows), 0) < lax.broadcasted_iota(
        jnp.int32, (rows, rows), 1
    )
    onehot = jnp.where(hit, 1.0, 0.0)
    counts = jnp.dot(
        onehot.astype(BF16), jnp.where(before, 1.0, 0.0).astype(BF16), preferred_element_type=F32
    )
    rank = jnp.sum(onehot * counts, axis=0, keepdims=True).astype(jnp.int32)
    target = dest_row * capacity + rank
    return lax.broadcasted_iota(jnp.int32, (slots, rows), 0) == target


def gather_kernel(offsets_ref, grad_ref, out_ref):
    length, slots = grad_ref.shape[0], offsets_ref.shape[1]
    pick = lax.broadcasted_iota(jnp.int32, (length, slots), 0) == offsets_ref[...]
    pick = jnp.where(pick, 1.0, 0.0).astype(BF16)
    out_ref[...] = lax.dot_general(
        pick, grad_ref[...], (((0,), (0,)), ((), ())), preferred_element_type=F32
    ).astype(BF16)


def owner_rows_kernel(groups, capacity, dest_ref, arrived_ref, token_ref, out_ref):
    slots = arrived_ref.shape[0]
    pick = rows_by_target(dest_ref[...], groups, capacity, slots)
    pick = jnp.where(pick, 1.0, 0.0).astype(BF16)
    rows = lax.dot_general(
        pick, arrived_ref[...], (((0,), (0,)), ((), ())), preferred_element_type=F32
    ).astype(BF16)
    out_ref[...] = rows


def route_kernel(groups, capacity, dest_ref, total_ref, last_ref, out_ref):
    slots = out_ref.shape[0]
    total = total_ref[...] + last_ref[...].astype(F32)
    hit = rows_by_target(dest_ref[...], groups, capacity, slots)
    pick = jnp.where(hit, 1.0, 0.0)
    sent = jnp.dot(pick.astype(BF16), total.astype(BF16), preferred_element_type=F32)
    used = jnp.sum(pick, axis=1, keepdims=True)
    out_ref[...] = jnp.where(used > 0.5, sent, EMPTY).astype(BF16)


def place_kernel(offsets_ref, arrived_ref, text_ref, out_ref):
    length, slots = text_ref.shape[0], offsets_ref.shape[1]
    arrived = arrived_ref[...].astype(F32)
    used = arrived[:, 0:1] < LIMIT
    rows = jnp.where(used, arrived, 0.0).astype(BF16)
    marks = jnp.where(jnp.broadcast_to(used, (slots, 128)), 1.0, 0.0).astype(BF16)
    pick = lax.broadcasted_iota(jnp.int32, (length, slots), 0) == offsets_ref[...]
    pick = jnp.where(pick, 1.0, 0.0).astype(BF16)
    placed = jnp.dot(pick, rows, preferred_element_type=F32)
    filled = jnp.dot(pick, marks, preferred_element_type=F32)[:, 0:1] > 0.5
    out_ref[...] = jnp.where(filled, placed, text_ref[...].astype(F32)).astype(BF16)


TRANS = (((1,), (1,)), ((), ()))


def fetch(at_ref, sources, held_ref, sems):
    blocks, width = held_ref.shape[1], held_ref.shape[3]
    copies = []
    for j in range(blocks):
        columns = pl.ds(pl.multiple_of(at_ref[j] * width, width), width)
        pair = []
        for k, source in enumerate(sources):
            pair.append(
                pltpu.make_async_copy(source.at[:, columns], held_ref.at[k, j], sems.at[k, j])
            )
            pair[-1].start()
        copies.append(pair)
    return copies


def forward_first_kernel(
    at_ref, own_ref, other_ref, w_own_ref, w_other_ref, out_ref, act_ref, held_ref, sems
):
    copies = fetch(at_ref, (w_own_ref, w_other_ref), held_ref, sems)
    half = own_ref.shape[1]
    act_ref[:, :half] = gelu(own_ref[...].astype(F32)).astype(BF16)
    act_ref[:, half:] = gelu(other_ref[...].astype(F32)).astype(BF16)
    for j, pair in enumerate(copies):
        for copy in pair:
            copy.wait()
        total = jnp.dot(act_ref[:, :half], held_ref[0, j], preferred_element_type=F32)
        total += jnp.dot(act_ref[:, half:], held_ref[1, j], preferred_element_type=F32)
        out_ref[j] = total.astype(BF16)


def forward_second_kernel(at_ref, act_ref, w_own_ref, w_other_ref, out_ref, held_ref, sems):
    copies = fetch(at_ref, (w_own_ref, w_other_ref), held_ref, sems)
    half = held_ref.shape[2]
    for j, pair in enumerate(copies):
        for copy in pair:
            copy.wait()
        total = jnp.dot(act_ref[:, :half], held_ref[0, j], preferred_element_type=F32)
        total += jnp.dot(act_ref[:, half:], held_ref[1, j], preferred_element_type=F32)
        out_ref[j] = total.astype(BF16)


def add_kernel(kept_ref, beside_ref, token_ref, total_ref, *term_refs):
    token_ref[...] = jnp.zeros_like(token_ref)
    total_ref[...] = kept_ref[0].astype(F32) + beside_ref[0].astype(F32)
    for j, term_ref in enumerate(term_refs, 1):
        total = kept_ref[j].astype(F32) + beside_ref[j].astype(F32)
        term_ref[...] = total.astype(term_ref.dtype)


def relay_kernel(held_ref, arrived_ref, total_ref, back_ref, out_ref, sum_ref):
    out_ref[...] = (held_ref[...] + arrived_ref[...].astype(F32)).astype(BF16)
    sum_ref[...] = total_ref[...] + back_ref[...].astype(F32)


def backward_first_kernel(blocks, at_ref, *refs):
    grad_refs, refs = refs[:blocks], refs[blocks:]
    pre_ref, w_own_ref, w_other_ref, own_ref, other_ref, slope_ref, held_ref, sems = refs
    copies = fetch(at_ref, (w_own_ref, w_other_ref), held_ref, sems)
    slope_ref[...] = gelu_slope(pre_ref[...].astype(F32))
    own, other = 0.0, 0.0
    for grad_ref, j, pair in zip(grad_refs, range(blocks), copies):
        for copy in pair:
            copy.wait()
        own += lax.dot_general(grad_ref[...], held_ref[0, j], TRANS, preferred_element_type=F32)
        other += lax.dot_general(grad_ref[...], held_ref[1, j], TRANS, preferred_element_type=F32)
    own_ref[...] = own
    other_ref[...] = other


def backward_second_kernel(
    at_ref, grad_ref, own_in, other_in, w_own_ref, w_other_ref, own_ref, other_ref, held_ref, sems
):
    copies = fetch(at_ref, (w_own_ref, w_other_ref), held_ref, sems)
    own, other = own_in[...], other_in[...]
    for j, pair in enumerate(copies):
        for copy in pair:
            copy.wait()
        own += lax.dot_general(grad_ref[j], held_ref[0, j], TRANS, preferred_element_type=F32)
        other += lax.dot_general(grad_ref[j], held_ref[1, j], TRANS, preferred_element_type=F32)
    own_ref[...] = own
    other_ref[...] = other.astype(BF16)


def slope_kernel(own_ref, other_ref, slope_ref, out_ref):
    total = own_ref[...] + other_ref[...].astype(F32)
    out_ref[...] = (total * slope_ref[...]).astype(BF16)


VMEM = pl.BlockSpec(memory_space=pltpu.VMEM)
HBM = pl.BlockSpec(memory_space=pltpu.HBM)
SMEM = pl.BlockSpec(memory_space=pltpu.SMEM)


def near_core(x):
    return pltpu.with_memory_space_constraint(x, pltpu.VMEM)


def in_hbm(x):
    return pltpu.with_memory_space_constraint(x, pltpu.HBM)


def call(kernel, outs, *args, final=False, first=False):
    out_shape = [jax.ShapeDtypeStruct(*o) if final else pltpu.VMEM(*o) for o in outs]
    got = pl.pallas_call(
        kernel,
        in_specs=[VMEM] * len(args),
        out_specs=[VMEM] * len(outs),
        out_shape=out_shape,
    )(*[a if first else near_core(a) for a in args])
    return got if len(outs) > 1 else got[0]


def product(kernel, outs, at, args, weights, blocks, share=1):
    hid, width = weights[0].shape[0], weights[0].shape[1] // (4 * blocks)
    rows = args[0].shape[-2]
    got = pl.pallas_call(
        kernel,
        in_specs=[SMEM] + [VMEM] * len(args) + [HBM] * 2,
        out_specs=[VMEM] * len(outs),
        out_shape=[pltpu.VMEM(*o) for o in outs],
        scratch_shapes=[
            pltpu.VMEM((2, blocks, hid, width), BF16),
            pltpu.SemaphoreType.DMA((2, blocks)),
        ],
        cost_estimate=pl.CostEstimate(
            flops=2 * rows * blocks * width * 2 * hid // share,
            bytes_accessed=4 * blocks * hid * width // share,
            transcendentals=0,
        ),
        compiler_params=pltpu.CompilerParams(vmem_limit_bytes=24 * 1024 * 1024),
    )(at, *[near_core(a) for a in args], *[in_hbm(w) for w in weights])
    return got if len(outs) > 1 else got[0]


def on_device(lines, pre_hidden, proj_weight, text_embed, routes_dest, place, grad_packed):
    groups = lax.axis_size("group")
    slots = place.shape[1]
    capacity = slots // groups
    rows, hid = pre_hidden.shape
    width = text_embed.shape[1]
    half = lines // 2
    line, core = lax.axis_index("line"), lax.axis_index("core")
    beside_line = line + 1 - 2 * lax.rem(line + core, 2) + lines
    steps = (2 - 4 * core) * jnp.arange(half, dtype=jnp.int32) + 2 * lines
    same = 2 * lax.rem(line + steps, lines) + core
    opposite = 2 * lax.rem(beside_line + steps, lines) + core
    dest_row = routes_dest.reshape(1, rows)

    cores = [(0, 1), (1, 0)]
    beside = []
    for i in range(lines):
        for c in range(2):
            odd = (i + c) % 2
            beside.append((2 * i + c, 2 * ((i + (-1 if odd else 1)) % lines) + c))

    def relay(x, by):
        pairs = []
        for i in range(lines):
            for c in range(2):
                pairs.append((2 * i + c, 2 * ((i + (by if c == 0 else -by)) % lines) + c))
        return lax.ppermute(x, ("line", "core"), pairs)

    def by_group(x):
        return x.reshape(groups, 4, capacity * width // 4)

    def exchange(x):
        x = lax.all_to_all(x, "group", split_axis=0, concat_axis=0, tiled=True)
        return x.reshape(slots, width)

    w_other = lax.ppermute(proj_weight, "core", cores)
    pre_other = lax.ppermute(pre_hidden, "core", cores)
    weights = (proj_weight, w_other)

    gathered = call(gather_kernel, [((slots, width), BF16)], place, grad_packed, first=True)
    returned = exchange(by_group(gathered))

    terms_out = ((half, rows, width), BF16)
    sent, act = product(
        forward_first_kernel,
        [terms_out, ((rows, 2 * hid), BF16)],
        opposite,
        (pre_hidden, pre_other),
        weights,
        half,
    )
    beside_terms = lax.ppermute(sent, ("line", "core"), beside)
    kept = product(forward_second_kernel, [terms_out], same, (act,), weights, half)
    token, total, first, second, third = call(
        add_kernel,
        [((8, 128), F32)] + [((rows, width), F32)] * 2 + [((rows, width), BF16)] * 2,
        kept,
        beside_terms,
    )
    passed = relay(second, 2)
    back = relay(third, -2)
    first, total = call(
        relay_kernel,
        [((rows, width), BF16), ((rows, width), F32)],
        first,
        passed,
        total,
        back,
    )
    last = relay(first, 2)
    outgoing = call(
        functools.partial(route_kernel, groups, capacity),
        [((slots, width), BF16)],
        dest_row,
        total,
        last,
    )
    outgoing = by_group(outgoing)
    arrived = exchange(outgoing)

    mine = call(
        functools.partial(owner_rows_kernel, groups, capacity),
        [((rows, width), BF16)],
        dest_row,
        returned,
        token,
    )
    last = relay(mine, 2)
    near = [mine, relay(mine, -2), relay(last, 2), last]
    far = lax.ppermute(jnp.stack(near), ("line", "core"), beside)
    wide = ((rows, hid), F32)
    own, other, slope = product(
        functools.partial(backward_first_kernel, half),
        [wide] * 3,
        same,
        (*near, pre_hidden),
        weights,
        half,
        1000,
    )
    own, other = product(
        backward_second_kernel,
        [wide, ((rows, hid), BF16)],
        opposite,
        (far, own, other),
        weights,
        half,
        1000,
    )
    other = lax.ppermute(other, "core", cores)
    grad_hidden = call(slope_kernel, [((rows, hid), BF16)], own, other, slope, final=True)

    packed = call(
        place_kernel, [(text_embed.shape, BF16)], place, arrived, text_embed, final=True
    )
    return (packed, grad_hidden)


def solution(mesh):
    groups, lines = mesh.shape["group"], mesh.shape["tensor"] // 2
    chips = Mesh(mesh.devices.reshape(groups, lines, 2), ("group", "line", "core"))
    tensor = ("line", "core")
    return jax.shard_map(
        functools.partial(on_device, lines),
        mesh=chips,
        in_specs=(
            P("group", tensor),
            P(tensor, None),
            P("group", tensor),
            P("group", None),
            P("group", None),
            P("group", tensor),
        ),
        out_specs=(P("group", tensor), P("group", tensor)),
        check_vma=False,
    )
```

```python
import functools

import jax
import jax.numpy as jnp
from jax import lax
from jax.experimental import pallas as pl
from jax.experimental.pallas import tpu as pltpu
from jax.sharding import Mesh
from jax.sharding import PartitionSpec as P

BF16 = jnp.bfloat16
F32 = jnp.float32
EMPTY = 1.7e38
LIMIT = 1.0e38


def gelu(values):
    return values * 0.5 * (1.0 + lax.erf(values * 0.7071067811865476))


def gelu_slope(values):
    cdf = 0.5 * (1.0 + lax.erf(values * 0.7071067811865476))
    dens = jnp.exp(-0.5 * values * values) * 0.3989422804014327
    return cdf + values * dens


def rows_by_target(dest_row, groups, capacity, slots):
    rows = dest_row.shape[1]
    hit = lax.broadcasted_iota(jnp.int32, (groups, rows), 0) == dest_row
    before = lax.broadcasted_iota(jnp.int32, (rows, rows), 0) < lax.broadcasted_iota(
        jnp.int32, (rows, rows), 1
    )
    onehot = jnp.where(hit, 1.0, 0.0)
    counts = jnp.dot(
        onehot.astype(BF16), jnp.where(before, 1.0, 0.0).astype(BF16), preferred_element_type=F32
    )
    rank = jnp.sum(onehot * counts, axis=0, keepdims=True).astype(jnp.int32)
    target = dest_row * capacity + rank
    return lax.broadcasted_iota(jnp.int32, (slots, rows), 0) == target


def gather_kernel(offsets_ref, grad_ref, out_ref):
    length, slots = grad_ref.shape[0], offsets_ref.shape[1]
    pick = lax.broadcasted_iota(jnp.int32, (length, slots), 0) == offsets_ref[...]
    pick = jnp.where(pick, 1.0, 0.0).astype(BF16)
    out_ref[...] = lax.dot_general(
        pick, grad_ref[...], (((0,), (0,)), ((), ())), preferred_element_type=F32
    ).astype(BF16)


def owner_rows_kernel(groups, capacity, dest_ref, arrived_ref, token_ref, out_ref):
    slots = arrived_ref.shape[0]
    pick = rows_by_target(dest_ref[...], groups, capacity, slots)
    pick = jnp.where(pick, 1.0, 0.0).astype(BF16)
    rows = lax.dot_general(
        pick, arrived_ref[...], (((0,), (0,)), ((), ())), preferred_element_type=F32
    ).astype(BF16)
    out_ref[...] = rows


def route_kernel(groups, capacity, dest_ref, total_ref, back_ref, last_ref, out_ref):
    slots = out_ref.shape[0]
    total = total_ref[...] + back_ref[...].astype(F32) + last_ref[...].astype(F32)
    hit = rows_by_target(dest_ref[...], groups, capacity, slots)
    pick = jnp.where(hit, 1.0, 0.0)
    sent = jnp.dot(pick.astype(BF16), total.astype(BF16), preferred_element_type=F32)
    used = jnp.sum(pick, axis=1, keepdims=True)
    out_ref[...] = jnp.where(used > 0.5, sent, EMPTY).astype(BF16)


def place_kernel(offsets_ref, arrived_ref, text_ref, out_ref):
    length, slots = text_ref.shape[0], offsets_ref.shape[1]
    arrived = arrived_ref[...].astype(F32)
    used = arrived[:, 0:1] < LIMIT
    rows = jnp.where(used, arrived, 0.0).astype(BF16)
    marks = jnp.where(jnp.broadcast_to(used, (slots, 128)), 1.0, 0.0).astype(BF16)
    pick = lax.broadcasted_iota(jnp.int32, (length, slots), 0) == offsets_ref[...]
    pick = jnp.where(pick, 1.0, 0.0).astype(BF16)
    placed = jnp.dot(pick, rows, preferred_element_type=F32)
    filled = jnp.dot(pick, marks, preferred_element_type=F32)[:, 0:1] > 0.5
    out_ref[...] = jnp.where(filled, placed, text_ref[...].astype(F32)).astype(BF16)


TRANS = (((1,), (1,)), ((), ()))


def fetch(at_ref, sources, held_ref, sems):
    blocks, width = held_ref.shape[1], held_ref.shape[3]
    copies = []
    for j in range(blocks):
        columns = pl.ds(pl.multiple_of(at_ref[j] * width, width), width)
        pair = []
        for k, source in enumerate(sources):
            pair.append(
                pltpu.make_async_copy(source.at[:, columns], held_ref.at[k, j], sems.at[k, j])
            )
            pair[-1].start()
        copies.append(pair)
    return copies


def forward_first_kernel(
    at_ref, own_ref, other_ref, w_own_ref, w_other_ref, out_ref, act_ref, held_ref, sems
):
    copies = fetch(at_ref, (w_own_ref, w_other_ref), held_ref, sems)
    half = own_ref.shape[1]
    act_ref[:, :half] = gelu(own_ref[...].astype(F32)).astype(BF16)
    act_ref[:, half:] = gelu(other_ref[...].astype(F32)).astype(BF16)
    for j, pair in enumerate(copies):
        for copy in pair:
            copy.wait()
        total = jnp.dot(act_ref[:, :half], held_ref[0, j], preferred_element_type=F32)
        total += jnp.dot(act_ref[:, half:], held_ref[1, j], preferred_element_type=F32)
        out_ref[j] = total.astype(BF16)


def forward_second_kernel(at_ref, act_ref, w_own_ref, w_other_ref, out_ref, held_ref, sems):
    copies = fetch(at_ref, (w_own_ref, w_other_ref), held_ref, sems)
    half = held_ref.shape[2]
    for j, pair in enumerate(copies):
        for copy in pair:
            copy.wait()
        total = jnp.dot(act_ref[:, :half], held_ref[0, j], preferred_element_type=F32)
        total += jnp.dot(act_ref[:, half:], held_ref[1, j], preferred_element_type=F32)
        out_ref[j] = total.astype(BF16)


def add_kernel(kept_ref, beside_ref, token_ref, total_ref, *term_refs):
    token_ref[...] = jnp.zeros_like(token_ref)
    total_ref[...] = kept_ref[0].astype(F32) + beside_ref[0].astype(F32)
    for j, term_ref in enumerate(term_refs, 1):
        total = kept_ref[j].astype(F32) + beside_ref[j].astype(F32)
        term_ref[...] = total.astype(term_ref.dtype)


def relay_kernel(held_ref, arrived_ref, out_ref):
    out_ref[...] = (held_ref[...] + arrived_ref[...].astype(F32)).astype(BF16)


def backward_first_kernel(blocks, at_ref, *refs):
    grad_refs, refs = refs[:blocks], refs[blocks:]
    pre_ref, w_own_ref, w_other_ref, own_ref, other_ref, slope_ref, held_ref, sems = refs
    copies = fetch(at_ref, (w_own_ref, w_other_ref), held_ref, sems)
    slope_ref[...] = gelu_slope(pre_ref[...].astype(F32))
    own, other = 0.0, 0.0
    for grad_ref, j, pair in zip(grad_refs, range(blocks), copies):
        for copy in pair:
            copy.wait()
        own += lax.dot_general(grad_ref[...], held_ref[0, j], TRANS, preferred_element_type=F32)
        other += lax.dot_general(grad_ref[...], held_ref[1, j], TRANS, preferred_element_type=F32)
    own_ref[...] = own
    other_ref[...] = other


def backward_second_kernel(
    at_ref, grad_ref, own_in, other_in, w_own_ref, w_other_ref, own_ref, other_ref, held_ref, sems
):
    copies = fetch(at_ref, (w_own_ref, w_other_ref), held_ref, sems)
    own, other = own_in[...], other_in[...]
    for j, pair in enumerate(copies):
        for copy in pair:
            copy.wait()
        own += lax.dot_general(grad_ref[j], held_ref[0, j], TRANS, preferred_element_type=F32)
        other += lax.dot_general(grad_ref[j], held_ref[1, j], TRANS, preferred_element_type=F32)
    own_ref[...] = own
    other_ref[...] = other.astype(BF16)


def slope_kernel(own_ref, other_ref, slope_ref, out_ref):
    total = own_ref[...] + other_ref[...].astype(F32)
    out_ref[...] = (total * slope_ref[...]).astype(BF16)


VMEM = pl.BlockSpec(memory_space=pltpu.VMEM)
HBM = pl.BlockSpec(memory_space=pltpu.HBM)
SMEM = pl.BlockSpec(memory_space=pltpu.SMEM)


def near_core(x):
    return pltpu.with_memory_space_constraint(x, pltpu.VMEM)


def in_hbm(x):
    return pltpu.with_memory_space_constraint(x, pltpu.HBM)


def call(kernel, outs, *args, final=False, first=False):
    out_shape = [jax.ShapeDtypeStruct(*o) if final else pltpu.VMEM(*o) for o in outs]
    got = pl.pallas_call(
        kernel,
        in_specs=[VMEM] * len(args),
        out_specs=[VMEM] * len(outs),
        out_shape=out_shape,
    )(*[a if first else near_core(a) for a in args])
    return got if len(outs) > 1 else got[0]


def product(kernel, outs, at, args, weights, blocks, share=1):
    hid, width = weights[0].shape[0], weights[0].shape[1] // (4 * blocks)
    rows = args[0].shape[-2]
    got = pl.pallas_call(
        kernel,
        in_specs=[SMEM] + [VMEM] * len(args) + [HBM] * 2,
        out_specs=[VMEM] * len(outs),
        out_shape=[pltpu.VMEM(*o) for o in outs],
        scratch_shapes=[
            pltpu.VMEM((2, blocks, hid, width), BF16),
            pltpu.SemaphoreType.DMA((2, blocks)),
        ],
        cost_estimate=pl.CostEstimate(
            flops=2 * rows * blocks * width * 2 * hid // share,
            bytes_accessed=4 * blocks * hid * width // share,
            transcendentals=0,
        ),
        compiler_params=pltpu.CompilerParams(vmem_limit_bytes=24 * 1024 * 1024),
    )(at, *[near_core(a) for a in args], *[in_hbm(w) for w in weights])
    return got if len(outs) > 1 else got[0]


def on_device(lines, pre_hidden, proj_weight, text_embed, routes_dest, place, grad_packed):
    groups = lax.axis_size("group")
    slots = place.shape[1]
    capacity = slots // groups
    rows, hid = pre_hidden.shape
    width = text_embed.shape[1]
    half = lines // 2
    line, core = lax.axis_index("line"), lax.axis_index("core")
    beside_line = line + 1 - 2 * lax.rem(line + core, 2) + lines
    steps = (2 - 4 * core) * jnp.arange(half, dtype=jnp.int32) + 2 * lines
    same = 2 * lax.rem(line + steps, lines) + core
    opposite = 2 * lax.rem(beside_line + steps, lines) + core
    dest_row = routes_dest.reshape(1, rows)

    cores = [(0, 1), (1, 0)]
    beside = []
    for i in range(lines):
        for c in range(2):
            odd = (i + c) % 2
            beside.append((2 * i + c, 2 * ((i + (-1 if odd else 1)) % lines) + c))

    def relay(x, by):
        pairs = []
        for i in range(lines):
            for c in range(2):
                pairs.append((2 * i + c, 2 * ((i + (by if c == 0 else -by)) % lines) + c))
        return lax.ppermute(x, ("line", "core"), pairs)

    def by_group(x):
        return x.reshape(groups, 4, capacity * width // 4)

    def exchange(x):
        x = lax.all_to_all(x, "group", split_axis=0, concat_axis=0, tiled=True)
        return x.reshape(slots, width)

    w_other = lax.ppermute(proj_weight, "core", cores)
    pre_other = lax.ppermute(pre_hidden, "core", cores)
    weights = (proj_weight, w_other)

    gathered = call(gather_kernel, [((slots, width), BF16)], place, grad_packed, first=True)
    returned = exchange(by_group(gathered))

    terms_out = ((half, rows, width), BF16)
    sent, act = product(
        forward_first_kernel,
        [terms_out, ((rows, 2 * hid), BF16)],
        opposite,
        (pre_hidden, pre_other),
        weights,
        half,
    )
    beside_terms = lax.ppermute(sent, ("line", "core"), beside)
    kept = product(forward_second_kernel, [terms_out], same, (act,), weights, half)
    token, total, first, second, third = call(
        add_kernel,
        [((8, 128), F32)] + [((rows, width), F32)] * 2 + [((rows, width), BF16)] * 2,
        kept,
        beside_terms,
    )
    passed = relay(second, 2)
    back = relay(third, -2)
    first = call(relay_kernel, [((rows, width), BF16)], first, passed)
    last = relay(first, 2)
    outgoing = call(
        functools.partial(route_kernel, groups, capacity),
        [((slots, width), BF16)],
        dest_row,
        total,
        back,
        last,
    )
    outgoing = by_group(outgoing)
    arrived = exchange(outgoing)

    mine = call(
        functools.partial(owner_rows_kernel, groups, capacity),
        [((rows, width), BF16)],
        dest_row,
        returned,
        token,
    )
    last = relay(mine, 2)
    near = [mine, relay(mine, -2), relay(last, 2), last]
    far = lax.ppermute(jnp.stack(near), ("line", "core"), beside)
    wide = ((rows, hid), F32)
    own, other, slope = product(
        functools.partial(backward_first_kernel, half),
        [wide] * 3,
        same,
        (*near, pre_hidden),
        weights,
        half,
        1000,
    )
    own, other = product(
        backward_second_kernel,
        [wide, ((rows, hid), BF16)],
        opposite,
        (far, own, other),
        weights,
        half,
        1000,
    )
    other = lax.ppermute(other, "core", cores)
    grad_hidden = call(slope_kernel, [((rows, hid), BF16)], own, other, slope, final=True)

    packed = call(
        place_kernel, [(text_embed.shape, BF16)], place, arrived, text_embed, final=True
    )
    return (packed, grad_hidden)


def solution(mesh):
    groups, lines = mesh.shape["group"], mesh.shape["tensor"] // 2
    chips = Mesh(mesh.devices.reshape(groups, lines, 2), ("group", "line", "core"))
    tensor = ("line", "core")
    return jax.shard_map(
        functools.partial(on_device, lines),
        mesh=chips,
        in_specs=(
            P("group", tensor),
            P(tensor, None),
            P("group", tensor),
            P("group", None),
            P("group", None),
            P("group", tensor),
        ),
        out_specs=(P("group", tensor), P("group", tensor)),
        check_vma=False,
    )
```

```python
import functools

import jax
import jax.numpy as jnp
from jax import lax
from jax.experimental import pallas as pl
from jax.experimental.pallas import tpu as pltpu
from jax.sharding import Mesh
from jax.sharding import PartitionSpec as P

BF16 = jnp.bfloat16
F32 = jnp.float32
EMPTY = 1.7e38
LIMIT = 1.0e38


def gelu(values):
    return values * 0.5 * (1.0 + lax.erf(values * 0.7071067811865476))


def gelu_slope(values):
    cdf = 0.5 * (1.0 + lax.erf(values * 0.7071067811865476))
    dens = jnp.exp(-0.5 * values * values) * 0.3989422804014327
    return cdf + values * dens


def rows_by_target(dest_row, groups, capacity, slots):
    rows = dest_row.shape[1]
    hit = lax.broadcasted_iota(jnp.int32, (groups, rows), 0) == dest_row
    before = lax.broadcasted_iota(jnp.int32, (rows, rows), 0) < lax.broadcasted_iota(
        jnp.int32, (rows, rows), 1
    )
    onehot = jnp.where(hit, 1.0, 0.0)
    counts = jnp.dot(
        onehot.astype(BF16), jnp.where(before, 1.0, 0.0).astype(BF16), preferred_element_type=F32
    )
    rank = jnp.sum(onehot * counts, axis=0, keepdims=True).astype(jnp.int32)
    target = dest_row * capacity + rank
    return lax.broadcasted_iota(jnp.int32, (slots, rows), 0) == target


def gather_kernel(offsets_ref, grad_ref, out_ref):
    length, slots = grad_ref.shape[0], offsets_ref.shape[1]
    pick = lax.broadcasted_iota(jnp.int32, (length, slots), 0) == offsets_ref[...]
    pick = jnp.where(pick, 1.0, 0.0).astype(BF16)
    out_ref[...] = lax.dot_general(
        pick, grad_ref[...], (((0,), (0,)), ((), ())), preferred_element_type=F32
    ).astype(BF16)


def owner_rows_kernel(groups, capacity, dest_ref, arrived_ref, token_ref, out_ref):
    slots = arrived_ref.shape[0]
    pick = rows_by_target(dest_ref[...], groups, capacity, slots)
    pick = jnp.where(pick, 1.0, 0.0).astype(BF16)
    rows = lax.dot_general(
        pick, arrived_ref[...], (((0,), (0,)), ((), ())), preferred_element_type=F32
    ).astype(BF16)
    out_ref[...] = rows


def route_kernel(groups, capacity, dest_ref, total_ref, back_ref, last_ref, out_ref):
    slots = out_ref.shape[0]
    total = total_ref[...] + back_ref[...].astype(F32) + last_ref[...].astype(F32)
    hit = rows_by_target(dest_ref[...], groups, capacity, slots)
    pick = jnp.where(hit, 1.0, 0.0)
    sent = jnp.dot(pick.astype(BF16), total.astype(BF16), preferred_element_type=F32)
    used = jnp.sum(pick, axis=1, keepdims=True)
    out_ref[...] = jnp.where(used > 0.5, sent, EMPTY).astype(BF16)


def place_kernel(offsets_ref, arrived_ref, text_ref, out_ref, token_ref):
    token_ref[...] = jnp.zeros_like(token_ref)
    length, slots = text_ref.shape[0], offsets_ref.shape[1]
    arrived = arrived_ref[...].astype(F32)
    used = arrived[:, 0:1] < LIMIT
    rows = jnp.where(used, arrived, 0.0).astype(BF16)
    marks = jnp.where(jnp.broadcast_to(used, (slots, 128)), 1.0, 0.0).astype(BF16)
    pick = lax.broadcasted_iota(jnp.int32, (length, slots), 0) == offsets_ref[...]
    pick = jnp.where(pick, 1.0, 0.0).astype(BF16)
    placed = jnp.dot(pick, rows, preferred_element_type=F32)
    filled = jnp.dot(pick, marks, preferred_element_type=F32)[:, 0:1] > 0.5
    out_ref[...] = jnp.where(filled, placed, text_ref[...].astype(F32)).astype(BF16)


TRANS = (((1,), (1,)), ((), ()))


def fetch(at_ref, sources, held_ref, sems):
    blocks, width = held_ref.shape[1], held_ref.shape[3]
    copies = []
    for j in range(blocks):
        columns = pl.ds(pl.multiple_of(at_ref[j] * width, width), width)
        pair = []
        for k, source in enumerate(sources):
            pair.append(
                pltpu.make_async_copy(source.at[:, columns], held_ref.at[k, j], sems.at[k, j])
            )
            pair[-1].start()
        copies.append(pair)
    return copies


def forward_first_kernel(
    at_ref, other_ref, w_own_ref, w_other_ref, own_ref, out_ref, act_ref, held_ref, sems
):
    half = other_ref.shape[1]
    own = pltpu.make_async_copy(own_ref, act_ref.at[:, :half], sems.at[2, 0])
    own.start()
    copies = fetch(at_ref, (w_own_ref, w_other_ref), held_ref, sems)
    act_ref[:, half:] = gelu(other_ref[...].astype(F32)).astype(BF16)
    own.wait()
    act_ref[:, :half] = gelu(act_ref[:, :half].astype(F32)).astype(BF16)
    for j, pair in enumerate(copies):
        for copy in pair:
            copy.wait()
        total = jnp.dot(act_ref[:, :half], held_ref[0, j], preferred_element_type=F32)
        total += jnp.dot(act_ref[:, half:], held_ref[1, j], preferred_element_type=F32)
        out_ref[j] = total.astype(BF16)


def forward_second_kernel(at_ref, act_ref, w_own_ref, w_other_ref, out_ref, held_ref, sems):
    copies = fetch(at_ref, (w_own_ref, w_other_ref), held_ref, sems)
    half = held_ref.shape[2]
    for j, pair in enumerate(copies):
        for copy in pair:
            copy.wait()
        total = jnp.dot(act_ref[:, :half], held_ref[0, j], preferred_element_type=F32)
        total += jnp.dot(act_ref[:, half:], held_ref[1, j], preferred_element_type=F32)
        out_ref[j] = total.astype(BF16)


def add_kernel(kept_ref, beside_ref, token_ref, total_ref, *term_refs):
    token_ref[...] = jnp.zeros_like(token_ref)
    total_ref[...] = kept_ref[0].astype(F32) + beside_ref[0].astype(F32)
    for j, term_ref in enumerate(term_refs, 1):
        total = kept_ref[j].astype(F32) + beside_ref[j].astype(F32)
        term_ref[...] = total.astype(term_ref.dtype)


def relay_kernel(held_ref, arrived_ref, out_ref):
    out_ref[...] = (held_ref[...] + arrived_ref[...].astype(F32)).astype(BF16)


def backward_first_kernel(blocks, at_ref, *refs):
    grad_refs, refs = refs[:blocks], refs[blocks:]
    pre_ref, w_own_ref, w_other_ref, own_ref, other_ref, slope_ref, held_ref, sems = refs
    copies = fetch(at_ref, (w_own_ref, w_other_ref), held_ref, sems)
    slope_ref[...] = gelu_slope(pre_ref[...].astype(F32))
    own, other = 0.0, 0.0
    for grad_ref, j, pair in zip(grad_refs, range(blocks), copies):
        for copy in pair:
            copy.wait()
        own += lax.dot_general(grad_ref[...], held_ref[0, j], TRANS, preferred_element_type=F32)
        other += lax.dot_general(grad_ref[...], held_ref[1, j], TRANS, preferred_element_type=F32)
    own_ref[...] = own
    other_ref[...] = other


def backward_second_kernel(
    at_ref, grad_ref, own_in, other_in, w_own_ref, w_other_ref, own_ref, other_ref, held_ref, sems
):
    copies = fetch(at_ref, (w_own_ref, w_other_ref), held_ref, sems)
    own, other = own_in[...], other_in[...]
    for j, pair in enumerate(copies):
        for copy in pair:
            copy.wait()
        own += lax.dot_general(grad_ref[j], held_ref[0, j], TRANS, preferred_element_type=F32)
        other += lax.dot_general(grad_ref[j], held_ref[1, j], TRANS, preferred_element_type=F32)
    own_ref[...] = own
    other_ref[...] = other.astype(BF16)


def slope_kernel(own_ref, other_ref, slope_ref, token_ref, out_ref):
    total = own_ref[...] + other_ref[...].astype(F32)
    out_ref[...] = (total * slope_ref[...]).astype(BF16)


VMEM = pl.BlockSpec(memory_space=pltpu.VMEM)
HBM = pl.BlockSpec(memory_space=pltpu.HBM)
SMEM = pl.BlockSpec(memory_space=pltpu.SMEM)


def near_core(x):
    return pltpu.with_memory_space_constraint(x, pltpu.VMEM)


def in_hbm(x):
    return pltpu.with_memory_space_constraint(x, pltpu.HBM)


def call(kernel, outs, *args, final=False, first=False):
    out_shape = [
        jax.ShapeDtypeStruct(*o) if final and i == 0 else pltpu.VMEM(*o)
        for i, o in enumerate(outs)
    ]
    got = pl.pallas_call(
        kernel,
        in_specs=[VMEM] * len(args),
        out_specs=[VMEM] * len(outs),
        out_shape=out_shape,
    )(*[a if first else near_core(a) for a in args])
    return got if len(outs) > 1 else got[0]


def product(kernel, outs, at, args, sources, blocks, share=1):
    hid, width = sources[0].shape[0], sources[0].shape[1] // (4 * blocks)
    rows = args[0].shape[-2]
    got = pl.pallas_call(
        kernel,
        in_specs=[SMEM] + [VMEM] * len(args) + [HBM] * len(sources),
        out_specs=[VMEM] * len(outs),
        out_shape=[pltpu.VMEM(*o) for o in outs],
        scratch_shapes=[
            pltpu.VMEM((2, blocks, hid, width), BF16),
            pltpu.SemaphoreType.DMA((3, blocks)),
        ],
        cost_estimate=pl.CostEstimate(
            flops=2 * rows * blocks * width * 2 * hid // share,
            bytes_accessed=4 * blocks * hid * width // share,
            transcendentals=0,
        ),
        compiler_params=pltpu.CompilerParams(vmem_limit_bytes=24 * 1024 * 1024),
    )(at, *[near_core(a) for a in args], *[in_hbm(x) for x in sources])
    return got if len(outs) > 1 else got[0]


def on_device(lines, pre_hidden, proj_weight, text_embed, routes_dest, place, grad_packed):
    groups = lax.axis_size("group")
    slots = place.shape[1]
    capacity = slots // groups
    rows, hid = pre_hidden.shape
    width = text_embed.shape[1]
    half = lines // 2
    line, core = lax.axis_index("line"), lax.axis_index("core")
    beside_line = line + 1 - 2 * lax.rem(line + core, 2) + lines
    steps = (2 - 4 * core) * jnp.arange(half, dtype=jnp.int32) + 2 * lines
    same = 2 * lax.rem(line + steps, lines) + core
    opposite = 2 * lax.rem(beside_line + steps, lines) + core
    dest_row = routes_dest.reshape(1, rows)

    cores = [(0, 1), (1, 0)]
    beside = []
    for i in range(lines):
        for c in range(2):
            odd = (i + c) % 2
            beside.append((2 * i + c, 2 * ((i + (-1 if odd else 1)) % lines) + c))

    def relay(x, by):
        pairs = []
        for i in range(lines):
            for c in range(2):
                pairs.append((2 * i + c, 2 * ((i + (by if c == 0 else -by)) % lines) + c))
        return lax.ppermute(x, ("line", "core"), pairs)

    def by_group(x):
        return x.reshape(groups, 4, capacity * width // 4)

    def exchange(x):
        x = lax.all_to_all(x, "group", split_axis=0, concat_axis=0, tiled=True)
        return x.reshape(slots, width)

    w_other = lax.ppermute(proj_weight, "core", cores)
    pre_other = lax.ppermute(pre_hidden, "core", cores)
    weights = (proj_weight, w_other)

    gathered = call(gather_kernel, [((slots, width), BF16)], place, grad_packed, first=True)
    returned = exchange(by_group(gathered))

    terms_out = ((half, rows, width), BF16)
    sent, act = product(
        forward_first_kernel,
        [terms_out, ((rows, 2 * hid), BF16)],
        opposite,
        (pre_other,),
        (*weights, pre_hidden),
        half,
    )
    beside_terms = lax.ppermute(sent, ("line", "core"), beside)
    kept = product(forward_second_kernel, [terms_out], same, (act,), weights, half)
    token, total, first, second, third = call(
        add_kernel,
        [((8, 128), F32)] + [((rows, width), F32)] * 2 + [((rows, width), BF16)] * 2,
        kept,
        beside_terms,
    )
    passed = relay(second, 2)
    back = relay(third, -2)
    first = call(relay_kernel, [((rows, width), BF16)], first, passed)
    last = relay(first, 2)
    outgoing = call(
        functools.partial(route_kernel, groups, capacity),
        [((slots, width), BF16)],
        dest_row,
        total,
        back,
        last,
    )
    outgoing = by_group(outgoing)
    arrived = exchange(outgoing)

    mine = call(
        functools.partial(owner_rows_kernel, groups, capacity),
        [((rows, width), BF16)],
        dest_row,
        returned,
        token,
    )
    last = relay(mine, 2)
    near = [mine, relay(mine, -2), relay(last, 2), last]
    far = lax.ppermute(jnp.stack(near), ("line", "core"), beside)
    wide = ((rows, hid), F32)
    own, other, slope = product(
        functools.partial(backward_first_kernel, half),
        [wide] * 3,
        same,
        (*near, pre_hidden),
        weights,
        half,
        1000,
    )
    own, other = product(
        backward_second_kernel,
        [wide, ((rows, hid), BF16)],
        opposite,
        (far, own, other),
        weights,
        half,
        1000,
    )
    other = lax.ppermute(other, "core", cores)
    packed, token = call(
        place_kernel,
        [(text_embed.shape, BF16), ((8, 128), F32)],
        place,
        arrived,
        text_embed,
        final=True,
    )
    grad_hidden = call(slope_kernel, [((rows, hid), BF16)], own, other, slope, token, final=True)
    return (packed, grad_hidden)


def solution(mesh):
    groups, lines = mesh.shape["group"], mesh.shape["tensor"] // 2
    chips = Mesh(mesh.devices.reshape(groups, lines, 2), ("group", "line", "core"))
    tensor = ("line", "core")
    return jax.shard_map(
        functools.partial(on_device, lines),
        mesh=chips,
        in_specs=(
            P("group", tensor),
            P(tensor, None),
            P("group", tensor),
            P("group", None),
            P("group", None),
            P("group", tensor),
        ),
        out_specs=(P("group", tensor), P("group", tensor)),
        check_vma=False,
    )
```

```python
import functools

import jax
import jax.numpy as jnp
from jax import lax
from jax.experimental import pallas as pl
from jax.experimental.pallas import tpu as pltpu
from jax.sharding import Mesh
from jax.sharding import PartitionSpec as P

BF16 = jnp.bfloat16
F32 = jnp.float32
EMPTY = 1.7e38
LIMIT = 1.0e38


def gelu(values):
    return values * 0.5 * (1.0 + lax.erf(values * 0.7071067811865476))


def gelu_slope(values):
    cdf = 0.5 * (1.0 + lax.erf(values * 0.7071067811865476))
    dens = jnp.exp(-0.5 * values * values) * 0.3989422804014327
    return cdf + values * dens


def rows_by_target(dest_row, groups, capacity, slots):
    rows = dest_row.shape[1]
    hit = lax.broadcasted_iota(jnp.int32, (groups, rows), 0) == dest_row
    before = lax.broadcasted_iota(jnp.int32, (rows, rows), 0) < lax.broadcasted_iota(
        jnp.int32, (rows, rows), 1
    )
    onehot = jnp.where(hit, 1.0, 0.0)
    counts = jnp.dot(
        onehot.astype(BF16), jnp.where(before, 1.0, 0.0).astype(BF16), preferred_element_type=F32
    )
    rank = jnp.sum(onehot * counts, axis=0, keepdims=True).astype(jnp.int32)
    target = dest_row * capacity + rank
    return lax.broadcasted_iota(jnp.int32, (slots, rows), 0) == target


def gather_kernel(offsets_ref, grad_ref, out_ref):
    length, slots = grad_ref.shape[0], offsets_ref.shape[1]
    pick = lax.broadcasted_iota(jnp.int32, (length, slots), 0) == offsets_ref[...]
    pick = jnp.where(pick, 1.0, 0.0).astype(BF16)
    out_ref[...] = lax.dot_general(
        pick, grad_ref[...], (((0,), (0,)), ((), ())), preferred_element_type=F32
    ).astype(BF16)


def owner_rows_kernel(groups, capacity, dest_ref, arrived_ref, token_ref, out_ref):
    slots = arrived_ref.shape[0]
    pick = rows_by_target(dest_ref[...], groups, capacity, slots)
    pick = jnp.where(pick, 1.0, 0.0).astype(BF16)
    rows = lax.dot_general(
        pick, arrived_ref[...], (((0,), (0,)), ((), ())), preferred_element_type=F32
    ).astype(BF16)
    out_ref[...] = rows


def route_kernel(groups, capacity, dest_ref, total_ref, back_ref, last_ref, out_ref):
    slots = out_ref.shape[0]
    total = total_ref[...] + back_ref[...].astype(F32) + last_ref[...].astype(F32)
    hit = rows_by_target(dest_ref[...], groups, capacity, slots)
    pick = jnp.where(hit, 1.0, 0.0)
    sent = jnp.dot(pick.astype(BF16), total.astype(BF16), preferred_element_type=F32)
    used = jnp.sum(pick, axis=1, keepdims=True)
    out_ref[...] = jnp.where(used > 0.5, sent, EMPTY).astype(BF16)


def place_kernel(offsets_ref, arrived_ref, text_ref, out_ref, token_ref):
    token_ref[...] = jnp.zeros_like(token_ref)
    length, slots = text_ref.shape[0], offsets_ref.shape[1]
    arrived = arrived_ref[...].astype(F32)
    used = arrived[:, 0:1] < LIMIT
    rows = jnp.where(used, arrived, 0.0).astype(BF16)
    marks = jnp.where(jnp.broadcast_to(used, (slots, 128)), 1.0, 0.0).astype(BF16)
    pick = lax.broadcasted_iota(jnp.int32, (length, slots), 0) == offsets_ref[...]
    pick = jnp.where(pick, 1.0, 0.0).astype(BF16)
    placed = jnp.dot(pick, rows, preferred_element_type=F32)
    filled = jnp.dot(pick, marks, preferred_element_type=F32)[:, 0:1] > 0.5
    out_ref[...] = jnp.where(filled, placed, text_ref[...].astype(F32)).astype(BF16)


TRANS = (((1,), (1,)), ((), ()))


WIDTHS = 16


def fetch(at_ref, sources, held_ref, sems):
    blocks, width = held_ref.shape[1], held_ref.shape[3]
    copies = []
    for j in range(blocks):
        columns = pl.ds(pl.multiple_of(at_ref[j] * width, width), width)
        pair = []
        for k, source in enumerate(sources):
            pair.append(
                pltpu.make_async_copy(source.at[:, columns], held_ref.at[k, j], sems.at[k, j])
            )
            pair[-1].start()
        copies.append(pair)
    return copies


def forward_first_kernel(
    at_ref, other_ref, w_own_ref, w_other_ref, own_ref, out_ref, act_ref, held_ref, sems
):
    half = other_ref.shape[1]
    own = pltpu.make_async_copy(own_ref, act_ref.at[:, :half], sems.at[2, 0])
    own.start()
    copies = fetch(at_ref, (w_own_ref, w_other_ref), held_ref, sems)
    act_ref[:, half:] = gelu(other_ref[...].astype(F32)).astype(BF16)
    own.wait()
    act_ref[:, :half] = gelu(act_ref[:, :half].astype(F32)).astype(BF16)
    for j, pair in enumerate(copies):
        for copy in pair:
            copy.wait()
        total = jnp.dot(act_ref[:, :half], held_ref[0, j], preferred_element_type=F32)
        total += jnp.dot(act_ref[:, half:], held_ref[1, j], preferred_element_type=F32)
        out_ref[j] = total.astype(BF16)


def forward_second_kernel(at_ref, act_ref, w_own_ref, w_other_ref, out_ref, held_ref, sems):
    copies = fetch(at_ref, (w_own_ref, w_other_ref), held_ref, sems)
    half = held_ref.shape[2]
    for j, pair in enumerate(copies):
        for copy in pair:
            copy.wait()
        total = jnp.dot(act_ref[:, :half], held_ref[0, j], preferred_element_type=F32)
        total += jnp.dot(act_ref[:, half:], held_ref[1, j], preferred_element_type=F32)
        out_ref[j] = total.astype(BF16)


def add_sent_kernel(kept_ref, beside_ref, second_ref, third_ref):
    for j, term_ref in enumerate((second_ref, third_ref)):
        total = kept_ref[2 + j].astype(F32) + beside_ref[j].astype(F32)
        term_ref[...] = total.astype(BF16)


def add_held_kernel(kept_ref, beside_ref, token_ref, total_ref, first_ref):
    token_ref[...] = jnp.zeros_like(token_ref)
    for j, term_ref in enumerate((total_ref, first_ref)):
        term_ref[...] = kept_ref[j].astype(F32) + beside_ref[j].astype(F32)


def relay_kernel(held_ref, arrived_ref, out_ref):
    out_ref[...] = (held_ref[...] + arrived_ref[...].astype(F32)).astype(BF16)


def backward_first_kernel(blocks, at_ref, *refs):
    grad_refs, refs = refs[:blocks], refs[blocks:]
    pre_ref, w_own_ref, w_other_ref, own_ref, other_ref, slope_ref, held_ref, sems = refs
    copies = fetch(at_ref, (w_own_ref, w_other_ref), held_ref, sems)
    slope_ref[...] = gelu_slope(pre_ref[...].astype(F32))
    own, other = 0.0, 0.0
    for grad_ref, j, pair in zip(grad_refs, range(blocks), copies):
        for copy in pair:
            copy.wait()
        own += lax.dot_general(grad_ref[...], held_ref[0, j], TRANS, preferred_element_type=F32)
        other += lax.dot_general(grad_ref[...], held_ref[1, j], TRANS, preferred_element_type=F32)
    own_ref[...] = own
    other_ref[...] = other


def backward_second_kernel(
    at_ref, grad_ref, own_in, other_in, w_own_ref, w_other_ref, own_ref, other_ref, held_ref, sems
):
    copies = fetch(at_ref, (w_own_ref, w_other_ref), held_ref, sems)
    own, other = own_in[...], other_in[...]
    for j, pair in enumerate(copies):
        for copy in pair:
            copy.wait()
        own += lax.dot_general(grad_ref[j], held_ref[0, j], TRANS, preferred_element_type=F32)
        other += lax.dot_general(grad_ref[j], held_ref[1, j], TRANS, preferred_element_type=F32)
    own_ref[...] = own
    other_ref[...] = other.astype(BF16)


def slope_kernel(own_ref, other_ref, slope_ref, token_ref, out_ref):
    total = own_ref[...] + other_ref[...].astype(F32)
    out_ref[...] = (total * slope_ref[...]).astype(BF16)


VMEM = pl.BlockSpec(memory_space=pltpu.VMEM)
HBM = pl.BlockSpec(memory_space=pltpu.HBM)
SMEM = pl.BlockSpec(memory_space=pltpu.SMEM)


def near_core(x):
    return pltpu.with_memory_space_constraint(x, pltpu.VMEM)


def in_hbm(x):
    return pltpu.with_memory_space_constraint(x, pltpu.HBM)


def call(kernel, outs, *args, final=False, first=False):
    out_shape = [
        jax.ShapeDtypeStruct(*o) if final and i == 0 else pltpu.VMEM(*o)
        for i, o in enumerate(outs)
    ]
    got = pl.pallas_call(
        kernel,
        in_specs=[VMEM] * len(args),
        out_specs=[VMEM] * len(outs),
        out_shape=out_shape,
    )(*[a if first else near_core(a) for a in args])
    return got if len(outs) > 1 else got[0]


def product(kernel, outs, at, args, sources, blocks, share=1):
    hid, width = sources[0].shape[0], sources[0].shape[1] // WIDTHS
    rows = args[0].shape[-2]
    got = pl.pallas_call(
        kernel,
        in_specs=[SMEM] + [VMEM] * len(args) + [HBM] * len(sources),
        out_specs=[VMEM] * len(outs),
        out_shape=[pltpu.VMEM(*o) for o in outs],
        scratch_shapes=[
            pltpu.VMEM((2, blocks, hid, width), BF16),
            pltpu.SemaphoreType.DMA((3, blocks)),
        ],
        cost_estimate=pl.CostEstimate(
            flops=2 * rows * blocks * width * 2 * hid // share,
            bytes_accessed=4 * blocks * hid * width // share,
            transcendentals=0,
        ),
        compiler_params=pltpu.CompilerParams(vmem_limit_bytes=24 * 1024 * 1024),
    )(at, *[near_core(a) for a in args], *[in_hbm(x) for x in sources])
    return got if len(outs) > 1 else got[0]


def on_device(lines, pre_hidden, proj_weight, text_embed, routes_dest, place, grad_packed):
    groups = lax.axis_size("group")
    slots = place.shape[1]
    capacity = slots // groups
    rows, hid = pre_hidden.shape
    width = text_embed.shape[1]
    half = lines // 2
    line, core = lax.axis_index("line"), lax.axis_index("core")
    beside_line = line + 1 - 2 * lax.rem(line + core, 2) + lines
    steps = (2 - 4 * core) * jnp.arange(half, dtype=jnp.int32) + 2 * lines
    same = 2 * lax.rem(line + steps, lines) + core
    opposite = 2 * lax.rem(beside_line + steps, lines) + core
    dest_row = routes_dest.reshape(1, rows)

    cores = [(0, 1), (1, 0)]
    beside = []
    for i in range(lines):
        for c in range(2):
            odd = (i + c) % 2
            beside.append((2 * i + c, 2 * ((i + (-1 if odd else 1)) % lines) + c))

    def relay(x, by):
        pairs = []
        for i in range(lines):
            for c in range(2):
                pairs.append((2 * i + c, 2 * ((i + (by if c == 0 else -by)) % lines) + c))
        return lax.ppermute(x, ("line", "core"), pairs)

    def by_group(x):
        return x.reshape(groups, 4, capacity * width // 4)

    def exchange(x):
        x = lax.all_to_all(x, "group", split_axis=0, concat_axis=0, tiled=True)
        return x.reshape(slots, width)

    w_other = lax.ppermute(proj_weight, "core", cores)
    pre_other = lax.ppermute(pre_hidden, "core", cores)
    weights = (proj_weight, w_other)

    gathered = call(gather_kernel, [((slots, width), BF16)], place, grad_packed, first=True)
    returned = exchange(by_group(gathered))

    terms_out = ((half, rows, width), BF16)
    two_out = ((2, rows, width), BF16)
    sent, act = product(
        forward_first_kernel,
        [two_out, ((rows, 2 * hid), BF16)],
        opposite[2:],
        (pre_other,),
        (*weights, pre_hidden),
        2,
    )
    beside_sent = lax.ppermute(sent, ("line", "core"), beside)
    held = product(forward_second_kernel, [two_out], opposite[:2], (act,), weights, 2)
    beside_held = lax.ppermute(held, ("line", "core"), beside)
    kept = product(forward_second_kernel, [terms_out], same, (act,), weights, half)
    second, third = call(add_sent_kernel, [((rows, width), BF16)] * 2, kept, beside_sent)
    token, total, first = call(
        add_held_kernel, [((8, 128), F32)] + [((rows, width), F32)] * 2, kept, beside_held
    )
    passed = relay(second, 2)
    back = relay(third, -2)
    first = call(relay_kernel, [((rows, width), BF16)], first, passed)
    last = relay(first, 2)
    outgoing = call(
        functools.partial(route_kernel, groups, capacity),
        [((slots, width), BF16)],
        dest_row,
        total,
        back,
        last,
    )
    outgoing = by_group(outgoing)
    arrived = exchange(outgoing)

    mine = call(
        functools.partial(owner_rows_kernel, groups, capacity),
        [((rows, width), BF16)],
        dest_row,
        returned,
        token,
    )
    last = relay(mine, 2)
    near = [mine, relay(mine, -2), relay(last, 2), last]
    far = lax.ppermute(jnp.stack(near), ("line", "core"), beside)
    wide = ((rows, hid), F32)
    own, other, slope = product(
        functools.partial(backward_first_kernel, half),
        [wide] * 3,
        same,
        (*near, pre_hidden),
        weights,
        half,
        1000,
    )
    own, other = product(
        backward_second_kernel,
        [wide, ((rows, hid), BF16)],
        opposite,
        (far, own, other),
        weights,
        half,
        1000,
    )
    other = lax.ppermute(other, "core", cores)
    packed, token = call(
        place_kernel,
        [(text_embed.shape, BF16), ((8, 128), F32)],
        place,
        arrived,
        text_embed,
        final=True,
    )
    grad_hidden = call(slope_kernel, [((rows, hid), BF16)], own, other, slope, token, final=True)
    return (packed, grad_hidden)


def solution(mesh):
    groups, lines = mesh.shape["group"], mesh.shape["tensor"] // 2
    chips = Mesh(mesh.devices.reshape(groups, lines, 2), ("group", "line", "core"))
    tensor = ("line", "core")
    return jax.shard_map(
        functools.partial(on_device, lines),
        mesh=chips,
        in_specs=(
            P("group", tensor),
            P(tensor, None),
            P("group", tensor),
            P("group", None),
            P("group", None),
            P("group", tensor),
        ),
        out_specs=(P("group", tensor), P("group", tensor)),
        check_vma=False,
    )
```

```python
import functools

import jax
import jax.numpy as jnp
from jax import lax
from jax.experimental import pallas as pl
from jax.experimental.pallas import tpu as pltpu
from jax.sharding import Mesh
from jax.sharding import PartitionSpec as P

BF16 = jnp.bfloat16
F32 = jnp.float32
EMPTY = 1.7e38
LIMIT = 1.0e38


def gelu(values):
    return values * 0.5 * (1.0 + lax.erf(values * 0.7071067811865476))


def gelu_slope(values):
    cdf = 0.5 * (1.0 + lax.erf(values * 0.7071067811865476))
    dens = jnp.exp(-0.5 * values * values) * 0.3989422804014327
    return cdf + values * dens


def rows_by_target(dest_row, groups, capacity, slots):
    rows = dest_row.shape[1]
    hit = lax.broadcasted_iota(jnp.int32, (groups, rows), 0) == dest_row
    before = lax.broadcasted_iota(jnp.int32, (rows, rows), 0) < lax.broadcasted_iota(
        jnp.int32, (rows, rows), 1
    )
    onehot = jnp.where(hit, 1.0, 0.0)
    counts = jnp.dot(
        onehot.astype(BF16), jnp.where(before, 1.0, 0.0).astype(BF16), preferred_element_type=F32
    )
    rank = jnp.sum(onehot * counts, axis=0, keepdims=True).astype(jnp.int32)
    target = dest_row * capacity + rank
    return lax.broadcasted_iota(jnp.int32, (slots, rows), 0) == target


def gather_kernel(offsets_ref, grad_ref, out_ref):
    length, slots = grad_ref.shape[0], offsets_ref.shape[1]
    pick = lax.broadcasted_iota(jnp.int32, (length, slots), 0) == offsets_ref[...]
    pick = jnp.where(pick, 1.0, 0.0).astype(BF16)
    out_ref[...] = lax.dot_general(
        pick, grad_ref[...], (((0,), (0,)), ((), ())), preferred_element_type=F32
    ).astype(BF16)


def owner_rows_kernel(groups, capacity, dest_ref, arrived_ref, token_ref, out_ref):
    slots = arrived_ref.shape[0]
    pick = rows_by_target(dest_ref[...], groups, capacity, slots)
    pick = jnp.where(pick, 1.0, 0.0).astype(BF16)
    rows = lax.dot_general(
        pick, arrived_ref[...], (((0,), (0,)), ((), ())), preferred_element_type=F32
    ).astype(BF16)
    out_ref[...] = rows


def route_kernel(groups, capacity, dest_ref, total_ref, back_ref, last_ref, out_ref):
    slots = out_ref.shape[0]
    total = total_ref[...] + back_ref[...].astype(F32) + last_ref[...].astype(F32)
    hit = rows_by_target(dest_ref[...], groups, capacity, slots)
    pick = jnp.where(hit, 1.0, 0.0)
    sent = jnp.dot(pick.astype(BF16), total.astype(BF16), preferred_element_type=F32)
    used = jnp.sum(pick, axis=1, keepdims=True)
    out_ref[...] = jnp.where(used > 0.5, sent, EMPTY).astype(BF16)


def place_kernel(offsets_ref, arrived_ref, text_ref, out_ref, token_ref):
    token_ref[...] = jnp.zeros_like(token_ref)
    length, slots = text_ref.shape[0], offsets_ref.shape[1]
    arrived = arrived_ref[...].astype(F32)
    used = arrived[:, 0:1] < LIMIT
    rows = jnp.where(used, arrived, 0.0).astype(BF16)
    marks = jnp.where(jnp.broadcast_to(used, (slots, 128)), 1.0, 0.0).astype(BF16)
    pick = lax.broadcasted_iota(jnp.int32, (length, slots), 0) == offsets_ref[...]
    pick = jnp.where(pick, 1.0, 0.0).astype(BF16)
    placed = jnp.dot(pick, rows, preferred_element_type=F32)
    filled = jnp.dot(pick, marks, preferred_element_type=F32)[:, 0:1] > 0.5
    out_ref[...] = jnp.where(filled, placed, text_ref[...].astype(F32)).astype(BF16)


TRANS = (((1,), (1,)), ((), ()))


def fetch(at_ref, sources, held_ref, sems, first=0):
    blocks, width = held_ref.shape[1], held_ref.shape[3]
    copies = []
    for j in range(blocks):
        columns = pl.ds(pl.multiple_of(at_ref[first + j] * width, width), width)
        pair = []
        for k, source in enumerate(sources):
            pair.append(
                pltpu.make_async_copy(source.at[:, columns], held_ref.at[k, j], sems.at[k, first + j])
            )
            pair[-1].start()
        copies.append(pair)
    return copies


def forward_first_kernel(
    at_ref, other_ref, w_own_ref, w_other_ref, own_ref, out_ref, act_ref, held_ref, sems
):
    half = other_ref.shape[1]
    own = pltpu.make_async_copy(own_ref, act_ref.at[:, :half], sems.at[2, 0])
    own.start()
    copies = fetch(at_ref, (w_own_ref, w_other_ref), held_ref, sems)
    act_ref[:, half:] = gelu(other_ref[...].astype(F32)).astype(BF16)
    own.wait()
    act_ref[:, :half] = gelu(act_ref[:, :half].astype(F32)).astype(BF16)
    for j, pair in enumerate(copies):
        for copy in pair:
            copy.wait()
        total = jnp.dot(act_ref[:, :half], held_ref[0, j], preferred_element_type=F32)
        total += jnp.dot(act_ref[:, half:], held_ref[1, j], preferred_element_type=F32)
        out_ref[j] = total.astype(BF16)


def forward_second_kernel(at_ref, act_ref, w_own_ref, w_other_ref, out_ref, held_ref, sems):
    copies = fetch(at_ref, (w_own_ref, w_other_ref), held_ref, sems)
    half = held_ref.shape[2]
    for j, pair in enumerate(copies):
        for copy in pair:
            copy.wait()
        total = jnp.dot(act_ref[:, :half], held_ref[0, j], preferred_element_type=F32)
        total += jnp.dot(act_ref[:, half:], held_ref[1, j], preferred_element_type=F32)
        out_ref[j] = total.astype(BF16)


def add_kernel(kept_ref, beside_ref, token_ref, total_ref, *term_refs):
    token_ref[...] = jnp.zeros_like(token_ref)
    total_ref[...] = kept_ref[0].astype(F32) + beside_ref[0].astype(F32)
    for j, term_ref in enumerate(term_refs, 1):
        total = kept_ref[j].astype(F32) + beside_ref[j].astype(F32)
        term_ref[...] = total.astype(term_ref.dtype)


def relay_kernel(held_ref, arrived_ref, out_ref):
    out_ref[...] = (held_ref[...] + arrived_ref[...].astype(F32)).astype(BF16)


def backward_first_kernel(blocks, at_ref, *refs):
    grad_refs, refs = refs[:blocks], refs[blocks:]
    pre_ref, w_own_ref, w_other_ref = refs[:3]
    own_ref, other_ref, slope_ref, next_ref, held_ref, sems = refs[3:]
    copies = fetch(at_ref, (w_own_ref, w_other_ref), held_ref, sems)
    later = fetch(at_ref, (w_own_ref, w_other_ref), next_ref, sems, blocks)
    slope_ref[...] = gelu_slope(pre_ref[...].astype(F32))
    own, other = 0.0, 0.0
    for grad_ref, j, pair in zip(grad_refs, range(blocks), copies):
        for copy in pair:
            copy.wait()
        own += lax.dot_general(grad_ref[...], held_ref[0, j], TRANS, preferred_element_type=F32)
        other += lax.dot_general(grad_ref[...], held_ref[1, j], TRANS, preferred_element_type=F32)
    own_ref[...] = own
    other_ref[...] = other
    for pair in later:
        for copy in pair:
            copy.wait()


def backward_second_kernel(grad_ref, own_in, other_in, held_ref, own_ref, other_ref):
    own, other = own_in[...], other_in[...]
    for j in range(grad_ref.shape[0]):
        own += lax.dot_general(grad_ref[j], held_ref[0, j], TRANS, preferred_element_type=F32)
        other += lax.dot_general(grad_ref[j], held_ref[1, j], TRANS, preferred_element_type=F32)
    own_ref[...] = own
    other_ref[...] = other.astype(BF16)


def slope_kernel(own_ref, other_ref, slope_ref, token_ref, out_ref):
    total = own_ref[...] + other_ref[...].astype(F32)
    out_ref[...] = (total * slope_ref[...]).astype(BF16)


VMEM = pl.BlockSpec(memory_space=pltpu.VMEM)
HBM = pl.BlockSpec(memory_space=pltpu.HBM)
SMEM = pl.BlockSpec(memory_space=pltpu.SMEM)


def near_core(x):
    return pltpu.with_memory_space_constraint(x, pltpu.VMEM)


def in_hbm(x):
    return pltpu.with_memory_space_constraint(x, pltpu.HBM)


def call(kernel, outs, *args, final=False, first=False):
    out_shape = [
        jax.ShapeDtypeStruct(*o) if final and i == 0 else pltpu.VMEM(*o)
        for i, o in enumerate(outs)
    ]
    got = pl.pallas_call(
        kernel,
        in_specs=[VMEM] * len(args),
        out_specs=[VMEM] * len(outs),
        out_shape=out_shape,
        compiler_params=pltpu.CompilerParams(vmem_limit_bytes=24 * 1024 * 1024),
    )(*[a if first else near_core(a) for a in args])
    return got if len(outs) > 1 else got[0]


def product(kernel, outs, at, args, sources, blocks, share=1):
    hid, width = sources[0].shape[0], sources[0].shape[1] // (4 * blocks)
    rows = args[0].shape[-2]
    got = pl.pallas_call(
        kernel,
        in_specs=[SMEM] + [VMEM] * len(args) + [HBM] * len(sources),
        out_specs=[VMEM] * len(outs),
        out_shape=[pltpu.VMEM(*o) for o in outs],
        scratch_shapes=[
            pltpu.VMEM((2, blocks, hid, width), BF16),
            pltpu.SemaphoreType.DMA((3, 2 * blocks)),
        ],
        cost_estimate=pl.CostEstimate(
            flops=2 * rows * blocks * width * 2 * hid // share,
            bytes_accessed=4 * blocks * hid * width // share,
            transcendentals=0,
        ),
        compiler_params=pltpu.CompilerParams(vmem_limit_bytes=24 * 1024 * 1024),
    )(at, *[near_core(a) for a in args], *[in_hbm(x) for x in sources])
    return got if len(outs) > 1 else got[0]


def on_device(lines, pre_hidden, proj_weight, text_embed, routes_dest, place, grad_packed):
    groups = lax.axis_size("group")
    slots = place.shape[1]
    capacity = slots // groups
    rows, hid = pre_hidden.shape
    width = text_embed.shape[1]
    half = lines // 2
    line, core = lax.axis_index("line"), lax.axis_index("core")
    beside_line = line + 1 - 2 * lax.rem(line + core, 2) + lines
    steps = (2 - 4 * core) * jnp.arange(half, dtype=jnp.int32) + 2 * lines
    same = 2 * lax.rem(line + steps, lines) + core
    opposite = 2 * lax.rem(beside_line + steps, lines) + core
    dest_row = routes_dest.reshape(1, rows)

    cores = [(0, 1), (1, 0)]
    beside = []
    for i in range(lines):
        for c in range(2):
            odd = (i + c) % 2
            beside.append((2 * i + c, 2 * ((i + (-1 if odd else 1)) % lines) + c))

    def relay(x, by):
        pairs = []
        for i in range(lines):
            for c in range(2):
                pairs.append((2 * i + c, 2 * ((i + (by if c == 0 else -by)) % lines) + c))
        return lax.ppermute(x, ("line", "core"), pairs)

    def by_group(x):
        return x.reshape(groups, 4, capacity * width // 4)

    def exchange(x):
        x = lax.all_to_all(x, "group", split_axis=0, concat_axis=0, tiled=True)
        return x.reshape(slots, width)

    w_other = lax.ppermute(proj_weight, "core", cores)
    pre_other = lax.ppermute(pre_hidden, "core", cores)
    weights = (proj_weight, w_other)

    gathered = call(gather_kernel, [((slots, width), BF16)], place, grad_packed, first=True)
    returned = exchange(by_group(gathered))

    terms_out = ((half, rows, width), BF16)
    sent, act = product(
        forward_first_kernel,
        [terms_out, ((rows, 2 * hid), BF16)],
        opposite,
        (pre_other,),
        (*weights, pre_hidden),
        half,
    )
    beside_terms = lax.ppermute(sent, ("line", "core"), beside)
    kept = product(forward_second_kernel, [terms_out], same, (act,), weights, half)
    token, total, first, second, third = call(
        add_kernel,
        [((8, 128), F32)] + [((rows, width), F32)] * 2 + [((rows, width), BF16)] * 2,
        kept,
        beside_terms,
    )
    passed = relay(second, 2)
    back = relay(third, -2)
    first = call(relay_kernel, [((rows, width), BF16)], first, passed)
    last = relay(first, 2)
    outgoing = call(
        functools.partial(route_kernel, groups, capacity),
        [((slots, width), BF16)],
        dest_row,
        total,
        back,
        last,
    )
    outgoing = by_group(outgoing)
    arrived = exchange(outgoing)

    mine = call(
        functools.partial(owner_rows_kernel, groups, capacity),
        [((rows, width), BF16)],
        dest_row,
        returned,
        token,
    )
    last = relay(mine, 2)
    near = [mine, relay(mine, -2), relay(last, 2), last]
    far = lax.ppermute(jnp.stack(near), ("line", "core"), beside)
    wide = ((rows, hid), F32)
    own, other, slope, held = product(
        functools.partial(backward_first_kernel, half),
        [wide] * 3 + [((2, half, hid, width), BF16)],
        jnp.concatenate([same, opposite]),
        (*near, pre_hidden),
        weights,
        half,
        1000,
    )
    own, other = call(
        backward_second_kernel, [wide, ((rows, hid), BF16)], far, own, other, held
    )
    other = lax.ppermute(other, "core", cores)
    packed, token = call(
        place_kernel,
        [(text_embed.shape, BF16), ((8, 128), F32)],
        place,
        arrived,
        text_embed,
        final=True,
    )
    grad_hidden = call(slope_kernel, [((rows, hid), BF16)], own, other, slope, token, final=True)
    return (packed, grad_hidden)


def solution(mesh):
    groups, lines = mesh.shape["group"], mesh.shape["tensor"] // 2
    chips = Mesh(mesh.devices.reshape(groups, lines, 2), ("group", "line", "core"))
    tensor = ("line", "core")
    return jax.shard_map(
        functools.partial(on_device, lines),
        mesh=chips,
        in_specs=(
            P("group", tensor),
            P(tensor, None),
            P("group", tensor),
            P("group", None),
            P("group", None),
            P("group", tensor),
        ),
        out_specs=(P("group", tensor), P("group", tensor)),
        check_vma=False,
    )
```
